256 devices in a mesh: recv: 32 (over x, z_lo, core), win: 8 (over y, z_hi).
Axes of the slice: x: 4, y: 4, z: 8 (z_hi: 2, z_lo: 4; z = z_hi * 4 + z_lo), core: 2. Of those that a mesh axis runs over, the one named last changes fastest.
Arguments:
- records: bfloat16 [512, 8, 2048], P('recv', 'win'), may hold values from -60 to 60, as said below
- usable: int32 [512, 8], P('recv', 'win'), may hold values from 0 to 1
- sources: int32 [128], replicated, may hold values from 0 to 511, as said below
Outputs:
- correlations: bfloat16 [128, 512, 512], P('win', 'recv')
The draws below stay inside these ranges and needn't reach their ends.
Inputs may be any that keep to these rules, and one draw needn't show every extreme that they name: Each entry of records is a finite sample. `sources`: 128 distinct channel indices.
All inputs are finite; a program needn't handle non-finite values.
Results may differ from the reference program's by a relative error of at most 0.0064.
Values may be sent and summed in bfloat16 or wider, within the bound.
No kernel may reach another device: no remote copies, remote signals or barrier semaphores. Data moves between devices by JAX's collectives and lax.ppermute only.
A program may use at most 64 MiB of HBM per device.

```python
import math
import jax
import jax.numpy as jnp
from jax import lax

L = 2048
HALF = 256
SMOOTH = 32
NS = 128
C = 512
W = 8


def draw_records(key, part):
    key = jax.random.fold_in(key, 1)
    key_noise, key_scale = jax.random.split(key, 2)
    scale = jnp.exp(jax.random.uniform(key_scale, (C, W, 1), jnp.float32, math.log(0.3), math.log(3.0)))
    values = jax.random.normal(key_noise, (C, W, L), jnp.float32) * scale
    return jnp.clip(values, -60.0, 60.0).astype(jnp.bfloat16)


def draw_usable(key, part):
    key = jax.random.fold_in(key, 2)
    key_dead, key_level, key_draw = jax.random.split(key, 3)
    dead_channel = jax.random.randint(key_dead, (C, 1), 0, 16) == 0
    level = jax.random.randint(key_level, (C, 1), 30, 96)
    rolled = jax.random.randint(key_draw, (C, W), 0, 100)
    return jnp.where((rolled < level) & jnp.logical_not(dead_channel), 1, 0).astype(jnp.int32)


def draw_sources(key, part):
    key = jax.random.fold_in(key, 3)
    key_pick, key_order = jax.random.split(key, 2)
    middle = jax.random.permutation(key_pick, C - 2)[:NS - 2].astype(jnp.int32) + 1
    chosen = jnp.concatenate([jnp.array([C - 1], jnp.int32), middle, jnp.array([0], jnp.int32)])
    order = jax.random.permutation(key_order, NS)
    return chosen[order].astype(jnp.int32)


def setup_inputs(seed: int = 0) -> dict:
    arg_keys = jax.random.split(jax.random.key(seed), 4)
    records = draw_records(jax.random.fold_in(arg_keys[3], 71), 0)
    usable = draw_usable(jax.random.fold_in(arg_keys[3], 71), 0)
    sources = draw_sources(jax.random.fold_in(arg_keys[3], 71), 0)
    return {"records": records, "usable": usable, "sources": sources}


def forward_table(length):
    bin_count = length // 2
    sample_ids = lax.broadcasted_iota(jnp.int32, (length, bin_count), 0)
    bin_ids = lax.broadcasted_iota(jnp.int32, (length, bin_count), 1)
    phases = (sample_ids * bin_ids % length).astype(jnp.float32) * (2.0 * math.pi / length)
    return jnp.concatenate([jnp.cos(phases), -jnp.sin(phases)], axis=1).astype(jnp.bfloat16)

def band_matrix(bin_count, reach):
    row_ids = lax.broadcasted_iota(jnp.int32, (bin_count, bin_count), 0)
    col_ids = lax.broadcasted_iota(jnp.int32, (bin_count, bin_count), 1)
    inside = (jnp.abs(row_ids - col_ids) <= reach).astype(jnp.float32)
    return inside / lax.optimization_barrier(jnp.sum(inside, axis=0, keepdims=True))

def inverse_table(length, lag_half):
    bin_count = length // 2
    bin_ids = lax.broadcasted_iota(jnp.int32, (bin_count, 2 * lag_half), 0)
    lag_ids = lax.broadcasted_iota(jnp.int32, (bin_count, 2 * lag_half), 1) - lag_half
    phases = (bin_ids * lag_ids % length).astype(jnp.float32) * (2.0 * math.pi / length)
    factor = jnp.where(bin_ids == 0, 1.0, 2.0).astype(jnp.float32) / math.sqrt(length)
    return jnp.concatenate([factor * jnp.cos(phases), -factor * jnp.sin(phases)], axis=0)

def whiten(flat_rows, dft_table, band_mean):
    widened = flat_rows.astype(jnp.float32)
    centred = (widened - lax.optimization_barrier(jnp.mean(widened, axis=-1, keepdims=True))).astype(jnp.bfloat16)
    spectrum = jnp.dot(centred, dft_table, preferred_element_type=jnp.float32)
    bin_half = spectrum.shape[-1] // 2
    real_part = spectrum[:, :bin_half]
    imag_part = spectrum[:, bin_half:]
    amplitude = jnp.sqrt(real_part * real_part + imag_part * imag_part)
    smooth = jnp.dot(amplitude, band_mean, precision=lax.Precision.HIGHEST)
    return spectrum / (jnp.concatenate([smooth, smooth], axis=1) + 1e-06)

def cross_term(src_block, src_weight, rec_spec, rec_weight):
    highest = lax.Precision.HIGHEST
    bin_half = src_block.shape[-1] // 2
    left_side = src_block * src_weight[:, :, None]
    right_side = rec_spec * rec_weight[:, :, None]
    left_re = left_side[..., :bin_half]
    left_im = left_side[..., bin_half:]
    right_re = right_side[..., :bin_half]
    right_im = right_side[..., bin_half:]
    real_part = jnp.einsum('nwf,cwf->ncf', left_re, right_re, precision=highest) + jnp.einsum('nwf,cwf->ncf', left_im, right_im, precision=highest)
    imag_part = jnp.einsum('nwf,cwf->ncf', left_im, right_re, precision=highest) - jnp.einsum('nwf,cwf->ncf', left_re, right_im, precision=highest)
    return jnp.concatenate([real_part, imag_part], axis=-1)

def reference(records, usable, sources):
    highest = lax.Precision.HIGHEST
    dft_table = forward_table(L)
    band_mean = band_matrix(L // 2, SMOOTH)
    inverse = inverse_table(L, HALF)
    whitened = whiten(records.reshape(C * W, L), dft_table, band_mean).reshape(C, W, L)
    rec_weight = usable.astype(jnp.float32)
    source_spec = whitened[sources]
    src_weight = rec_weight[sources]
    pair_count = jnp.dot(src_weight, rec_weight.T, precision=highest)
    per_block = min(NS, 16)
    block_total = NS // per_block

    def one_block(pieces):
        spec_block, weight_block, count_block = pieces
        spectra = cross_term(spec_block, weight_block, whitened, rec_weight)
        lagged = jnp.dot(spectra, inverse, precision=highest)
        return (lagged / jnp.sqrt(jnp.maximum(count_block, 1.0))[:, :, None]).astype(jnp.bfloat16)
    result = lax.map(one_block, (source_spec.reshape(block_total, per_block, W, L), src_weight.reshape(block_total, per_block, W), pair_count.reshape(block_total, per_block, C)))
    return result.reshape(NS, C, 2 * HALF)
```

```python
import functools
import math

import jax
import jax.numpy as jnp
import numpy as np
from jax import lax
from jax.experimental import pallas as pl
from jax.experimental.pallas import tpu as pltpu
from jax.sharding import Mesh
from jax.sharding import PartitionSpec as P

LENGTH = 2048
BINS = LENGTH // 2
HALF = 256
LAGS = 2 * HALF
SMOOTH = 32
LANES = 128
SLICES = LENGTH // LANES
BLOCKS = BINS // LANES
WINS = 8
OWN = 16
SOURCES = 128
CHANNELS = 512
MARK = 1e30
MARK_LIMIT = 1e29
BF16 = jnp.bfloat16
F32 = jnp.float32


def forward_table():
    samples = np.arange(LENGTH)[:, None]
    bins = np.arange(BINS)[None, :]
    phases = (samples * bins % LENGTH).astype(np.float32) * np.float32(2.0 * math.pi / LENGTH)
    table = np.stack([np.cos(phases), -np.sin(phases)], axis=1).reshape(LENGTH, 2, BLOCKS, LANES)
    return table.transpose(2, 0, 1, 3).reshape(BLOCKS, LENGTH, 2 * LANES).astype(jnp.bfloat16)


def inverse_table():
    bins = np.arange(BINS)[:, None]
    lags = np.arange(LAGS)[None, :] - HALF
    phases = (bins * lags % LENGTH).astype(np.float32) * np.float32(2.0 * math.pi / LENGTH)
    factor = np.where(bins == 0, 1.0, 2.0).astype(np.float32) / np.float32(math.sqrt(LENGTH))
    table = np.stack([factor * np.cos(phases), -factor * np.sin(phases)], axis=0)
    table = table.reshape(2, BLOCKS, LANES, LAGS).transpose(1, 0, 2, 3)
    return table.reshape(LENGTH, LAGS).astype(jnp.bfloat16)


def band_table():
    rows = np.arange(3 * LANES)[:, None] - LANES
    cols = np.arange(LANES)[None, :]
    return (np.abs(rows - cols) <= SMOOTH).astype(np.float32).astype(jnp.bfloat16)


def band_share():
    bins = np.arange(BINS)
    count = np.minimum(bins, SMOOTH) + np.minimum(BINS - 1 - bins, SMOOTH) + 1
    share = (1.0 / count).astype(np.float32).reshape(BLOCKS, 1, LANES)
    return np.broadcast_to(share, (BLOCKS, 8, LANES)).copy()


def centre_kernel(records_ref, usable_ref, slices_ref, rows_ref):
    widened = records_ref[...].astype(F32)
    mean = jnp.sum(widened, axis=1, keepdims=True) * (1.0 / LENGTH)
    centred = widened - mean
    row_ids = lax.broadcasted_iota(jnp.int32, (OWN, OWN), 0)
    col_ids = lax.broadcasted_iota(jnp.int32, (OWN, OWN), 1)
    flags = jnp.broadcast_to(usable_ref[...].astype(F32), (OWN, OWN))
    flag = jnp.sum(jnp.where(row_ids == col_ids, flags, 0.0), axis=1, keepdims=True)
    marked = jnp.where(flag > 0.5, centred, MARK).astype(BF16)
    rows_ref[...] = marked
    for part in range(SLICES):
        piece = marked[:, part * LANES : (part + 1) * LANES]
        slices_ref[2 * part] = piece
        slices_ref[2 * part + 1] = piece


def pick_kernel(sources_ref, all_ref, picked_ref):
    core = lax.axis_index("core")
    rows = all_ref[...].reshape(CHANNELS, LANES)
    channel_ids = lax.broadcasted_iota(jnp.int32, (CHANNELS, SOURCES), 0)
    onehot = (channel_ids == sources_ref[...]).astype(F32).astype(BF16)
    picked = lax.dot_general(
        onehot, rows, (((0,), (0,)), ((), ())), preferred_element_type=F32
    ).reshape(WINS, 2, 8, LANES)
    half = jnp.where(core == 0, picked[:, 0], picked[:, 1]).astype(BF16)
    for place in range(SLICES):
        picked_ref[pl.ds(place * WINS, WINS)] = half


def unmark(values):
    return jnp.where(values.astype(F32) > MARK_LIMIT, 0.0, values.astype(F32)).astype(BF16)


def correlate_kernel(
    own_ref, other_ref, rec_ref, table_ref, band_ref, share_ref, inverse_ref, out_ref,
    rows, spec, amp, cross,
):
    core = lax.axis_index("core")
    side = lax.axis_index("zh")
    for part in range(SLICES):
        lanes = pl.ds(part * LANES, LANES)
        rows[0:64, lanes] = unmark(own_ref[part].reshape(64, LANES))
        rows[64:128, lanes] = unmark(other_ref[part].reshape(64, LANES))
    rec_flags = []
    for win in range(WINS):
        slot = (win // 2) * 2 + (win % 2 + side) % 2
        received = rec_ref[slot]
        rows[pl.ds(128 + win * OWN, OWN), :] = unmark(received)
        rec_flags.append((received[:, :LANES].astype(F32) < MARK_LIMIT).astype(F32))

    for block in range(BLOCKS):
        part = jnp.dot(rows[...], table_ref[block], preferred_element_type=F32)
        spec[block] = part
        real, imag = part[:, :LANES], part[:, LANES:]
        amp[:, pl.ds(block * LANES, LANES)] = jnp.sqrt(real * real + imag * imag).astype(BF16)

    for block in range(BLOCKS):
        first, last = max(block - 1, 0), min(block + 2, BLOCKS)
        offset = (first - block + 1) * LANES
        width = (last - first) * LANES
        total = jnp.dot(
            amp[:, pl.ds(first * LANES, width)],
            band_ref[pl.ds(offset, width), :],
            preferred_element_type=F32,
        )
        scale = 1.0 / (total * share_ref[block, 0:1, :] + 1e-6)
        spec[block, :, :LANES] = spec[block, :, :LANES] * scale
        spec[block, :, LANES:] = spec[block, :, LANES:] * scale

    def one_block(block, carry):
        rec_re = [spec[block, pl.ds(128 + w * OWN, OWN), :LANES] for w in range(WINS)]
        rec_im = [spec[block, pl.ds(128 + w * OWN, OWN), LANES:] for w in range(WINS)]
        for index in range(OWN):
            base = (index // 8) * 64 + index % 8
            real = imag = None
            for w in range(WINS):
                row = base + w * 8
                src_re = jnp.broadcast_to(spec[block, row : row + 1, :LANES], (OWN, LANES))
                src_im = jnp.broadcast_to(spec[block, row : row + 1, LANES:], (OWN, LANES))
                re_part = src_re * rec_re[w] + src_im * rec_im[w]
                im_part = src_im * rec_re[w] - src_re * rec_im[w]
                real = re_part if real is None else real + re_part
                imag = im_part if imag is None else imag + im_part
            cross[block, pl.ds(index * OWN, OWN), :LANES] = real.astype(BF16)
            cross[block, pl.ds(index * OWN, OWN), LANES:] = imag.astype(BF16)
        return carry

    lax.fori_loop(0, BLOCKS, one_block, 0)

    lagged = jnp.dot(cross[0], inverse_ref[0 : 2 * LANES, :], preferred_element_type=F32)
    for block in range(1, BLOCKS):
        lagged += jnp.dot(
            cross[block], inverse_ref[pl.ds(block * 2 * LANES, 2 * LANES), :], preferred_element_type=F32
        )
    for which, ref in enumerate((own_ref, other_ref)):
        half = jnp.where(which == 0, core, 1 - core) * 8
        flags = (ref[0].astype(F32) < MARK_LIMIT).astype(F32)
        for index in range(8):
            count = jnp.zeros((OWN, LANES), F32)
            for w in range(WINS):
                count += jnp.broadcast_to(flags[w, index : index + 1, :], (OWN, LANES)) * rec_flags[w]
            scale = lax.rsqrt(jnp.maximum(count, 1.0))
            pair = (which * 8 + index) * OWN
            for piece in range(LAGS // LANES):
                lanes = slice(piece * LANES, (piece + 1) * LANES)
                out_ref[half + index, :, lanes] = (lagged[pair : pair + OWN, lanes] * scale).astype(BF16)


def local(records, usable, sources):
    rows_in = records.reshape(OWN, LENGTH)
    slices, rows = pl.pallas_call(
        centre_kernel,
        out_shape=(
            jax.ShapeDtypeStruct((2 * SLICES, OWN, LANES), BF16),
            jax.ShapeDtypeStruct((OWN, LENGTH), BF16),
        ),
    )(rows_in, usable.reshape(1, OWN))
    all_channels = lax.all_to_all(slices, ("x", "z", "core"), 0, 0)
    opposite = lax.ppermute(rows, "zh", [(0, 1), (1, 0)])
    received = lax.all_gather(jnp.concatenate([rows, opposite], axis=0), "y", axis=0)
    picked = pl.pallas_call(
        pick_kernel,
        out_shape=jax.ShapeDtypeStruct((SLICES * WINS, 8, LANES), BF16),
    )(sources.reshape(1, SOURCES), all_channels)
    own = lax.all_to_all(picked, ("x", "z", "y", "zh"), 0, 0)
    other = lax.ppermute(own, "core", [(0, 1), (1, 0)])
    own = own.reshape(SLICES, WINS, 8, LANES)
    other = other.reshape(SLICES, WINS, 8, LANES)
    return pl.pallas_call(
        correlate_kernel,
        out_shape=jax.ShapeDtypeStruct((OWN, OWN, LAGS), BF16),
        scratch_shapes=[
            pltpu.VMEM((256, LENGTH), BF16),
            pltpu.VMEM((BLOCKS, 256, 2 * LANES), F32),
            pltpu.VMEM((256, BINS), BF16),
            pltpu.VMEM((BLOCKS, 256, 2 * LANES), BF16),
        ],
        compiler_params=pltpu.CompilerParams(vmem_limit_bytes=40 * 2**20),
    )(
        own,
        other,
        received.reshape(WINS, OWN, LENGTH),
        jnp.asarray(forward_table()),
        jnp.asarray(band_table()),
        jnp.asarray(band_share()),
        jnp.asarray(inverse_table()),
    )


def solution(mesh):
    split = Mesh(mesh.devices.reshape(4, 4, 2, 4, 2), ("x", "z", "core", "y", "zh"))
    recv, win = ("x", "z", "core"), ("y", "zh")
    in_specs = (P(recv, win, None), P(recv, win), P())
    out_specs = P(win, recv, None)
    return jax.shard_map(local, mesh=split, in_specs=in_specs, out_specs=out_specs, check_vma=False)
```

```python
import functools
import math

import jax
import jax.numpy as jnp
import numpy as np
from jax import lax
from jax.experimental import pallas as pl
from jax.experimental.pallas import tpu as pltpu
from jax.sharding import Mesh
from jax.sharding import PartitionSpec as P

LENGTH = 2048
BINS = LENGTH // 2
FOLD = LENGTH // 2
HALF = 256
LAGS = 2 * HALF
SMOOTH = 32
LANES = 128
SLICES = LENGTH // LANES
BLOCKS = BINS // LANES
WINS = 8
OWN = 16
SOURCES = 128
CHANNELS = 512
HELD = WINS * 8
MARK = 1e30
MARK_LIMIT = 1e29
BF16 = jnp.bfloat16
VMEM_SPEC = pl.BlockSpec(memory_space=pltpu.VMEM)
HBM_SPEC = pl.BlockSpec(memory_space=pltpu.HBM)
F32 = jnp.float32


def bin_order():
    return np.concatenate([np.arange(0, BINS, 2), np.arange(1, BINS, 2)])


def forward_table():
    samples = np.arange(FOLD)[:, None]
    phases = (samples * bin_order()[None, :] % LENGTH).astype(np.float32) * np.float32(2.0 * math.pi / LENGTH)
    table = np.stack([np.cos(phases), -np.sin(phases)], axis=1).reshape(FOLD, 2, BLOCKS, LANES)
    return table.transpose(2, 0, 1, 3).reshape(BLOCKS, FOLD, 2 * LANES).astype(jnp.bfloat16)


def inverse_table():
    bins = bin_order()[:, None]
    lags = np.arange(LAGS)[None, :] - HALF
    phases = (bins * lags % LENGTH).astype(np.float32) * np.float32(2.0 * math.pi / LENGTH)
    factor = np.where(bins == 0, 1.0, 2.0).astype(np.float32) / np.float32(math.sqrt(LENGTH))
    table = np.stack([factor * np.cos(phases), -factor * np.sin(phases)], axis=0)
    table = table.reshape(2, BLOCKS, LANES, LAGS).transpose(1, 0, 2, 3)
    return table.reshape(BLOCKS, 2 * LANES, LAGS).astype(jnp.bfloat16)


def centre_kernel(records_ref, usable_ref, slices_ref, rows_ref):
    widened = records_ref[...].astype(F32)
    mean = jnp.sum(widened, axis=1, keepdims=True) * (1.0 / LENGTH)
    centred = widened - mean
    row_ids = lax.broadcasted_iota(jnp.int32, (OWN, OWN), 0)
    col_ids = lax.broadcasted_iota(jnp.int32, (OWN, OWN), 1)
    flags = jnp.broadcast_to(usable_ref[...].astype(F32), (OWN, OWN))
    flag = jnp.sum(jnp.where(row_ids == col_ids, flags, 0.0), axis=1, keepdims=True)
    marked = jnp.where(flag > 0.5, centred, MARK).astype(BF16)
    rows_ref[...] = marked
    for part in range(SLICES):
        piece = marked[:, part * LANES : (part + 1) * LANES]
        slices_ref[2 * part] = piece
        slices_ref[2 * part + 1] = piece


def pick_kernel(sources_ref, all_ref, rows_ref, opposite_ref, picked_ref, pair_ref, token_ref):
    pair_ref[:OWN] = rows_ref[...]
    pair_ref[OWN:] = opposite_ref[...]
    core = lax.axis_index("core")
    rows = all_ref[...].reshape(CHANNELS, LANES)
    channel_ids = lax.broadcasted_iota(jnp.int32, (CHANNELS, SOURCES), 0)
    onehot = (channel_ids == sources_ref[...]).astype(F32).astype(BF16)
    picked = lax.dot_general(
        onehot, rows, (((0,), (0,)), ((), ())), preferred_element_type=F32
    ).reshape(WINS, 2, 8, LANES)
    half = jnp.where(core == 0, picked[:, 0], picked[:, 1]).astype(BF16)
    for place in range(SLICES):
        picked_ref[pl.ds(place * WINS, WINS)] = half
    token_ref[...] = jnp.zeros((8, LANES), F32)


def load_kernel(token_ref, table_hbm, table_ref, sem):
    del token_ref
    copy = pltpu.make_async_copy(table_hbm, table_ref, sem)
    copy.start()
    copy.wait()


def unmark(values):
    widened = values.astype(F32)
    return jnp.where(widened > MARK_LIMIT, 0.0, widened)


def usable_lanes(values):
    return (values.astype(F32) < MARK_LIMIT).astype(F32)


def store_folded(even, odd, where, lanes, low, high):
    low, high = unmark(low), unmark(high)
    even[where, lanes] = (low + high).astype(BF16)
    odd[where, lanes] = (low - high).astype(BF16)


def store_sources(ref, even, odd):
    for part in range(SLICES // 2):
        low = ref[part].reshape(HELD, LANES)
        high = ref[part + SLICES // 2].reshape(HELD, LANES)
        store_folded(even, odd, pl.ds(0, HELD), pl.ds(part * LANES, LANES), low, high)


def band_matrices():
    rows = lax.broadcasted_iota(jnp.int32, (2 * LANES, 2 * LANES), 0)
    cols = lax.broadcasted_iota(jnp.int32, (2 * LANES, 2 * LANES), 1)
    apart = 2 * (rows - cols)
    return {
        (shift, step): (jnp.abs(apart + shift + 4 * LANES * step) <= SMOOTH).astype(F32).astype(BF16)
        for shift in (-1, 0, 1)
        for step in (-1, 0, 1)
    }


def whiten(even, odd, even_table, odd_table, spec, amp, before_odd):
    bands = band_matrices()
    for block in range(BLOCKS):
        if block == BLOCKS // 2:
            before_odd()
        folded, table = (even, even_table) if block < BLOCKS // 2 else (odd, odd_table)
        part = jnp.dot(folded[...], table[block % (BLOCKS // 2)], preferred_element_type=F32)
        spec[block] = part
        real, imag = part[:, :LANES], part[:, LANES:]
        amp[:, pl.ds(block * LANES, LANES)] = jnp.sqrt(real * real + imag * imag).astype(BF16)

    lane_ids = lax.broadcasted_iota(jnp.int32, (1, 2 * LANES), 1)
    for pair in range(BLOCKS // 2):
        parity, place = divmod(pair, 2)
        total = None
        for other in range(4):
            near = jnp.dot(
                amp[:, pl.ds(other * 2 * LANES, 2 * LANES)],
                bands[other // 2 - parity, other % 2 - place],
                preferred_element_type=F32,
            )
            total = near if total is None else total + near
        bin_ids = 2 * (lane_ids + place * 2 * LANES) + parity
        count = jnp.minimum(bin_ids, SMOOTH) + jnp.minimum(BINS - 1 - bin_ids, SMOOTH) + 1
        scale = 1.0 / (total * (1.0 / count.astype(F32)) + 1e-6)
        for half in range(2):
            block = 2 * pair + half
            piece = scale[:, half * LANES : (half + 1) * LANES]
            spec[block, :, :LANES] = spec[block, :, :LANES] * piece
            spec[block, :, LANES:] = spec[block, :, LANES:] * piece


def whiten_kernel(
    own_ref, pair_ref, next1_ref, next2_ref, next3_ref, even_table, odd_hbm,
    spec, send, flags, odd_table, even, odd, amp, sem,
):
    odd_copy = pltpu.make_async_copy(odd_hbm, odd_table, sem)
    odd_copy.start()
    line = lax.axis_index("y")
    side = lax.axis_index("zh")
    store_sources(own_ref, even, odd)
    for step, ref in enumerate((pair_ref, next1_ref, next2_ref, next3_ref)):
        for swap in range(2):
            win = lax.rem(line + 4 - step, 4) * 2 + lax.rem(side + swap, 2)
            first = pl.multiple_of(win * OWN, OWN)
            received = ref[swap * OWN : swap * OWN + OWN, :]
            where = pl.ds(HELD + first, OWN)
            store_folded(even, odd, where, slice(None), received[:, :FOLD], received[:, FOLD:])
            flags[pl.ds(first, OWN), :] = usable_lanes(received[:, :LANES])
    whiten(even, odd, even_table, odd_table, spec, amp, odd_copy.wait)
    send[:BLOCKS] = spec[:, :HELD, :].astype(BF16)
    usable = usable_lanes(own_ref[0].reshape(HELD, LANES)).astype(BF16)
    send[BLOCKS, :, :LANES] = usable
    send[BLOCKS, :, LANES:] = usable


def correlate(sources, flags, ready, rec_flags, inverse, store, held, added, cross, before_inverse):
    held[...] = sources[:BLOCKS].astype(F32)
    added[...] = held[:, :, :LANES] + held[:, :, LANES:]

    def one_block(block, carry):
        for part in range(0, OWN, 8):
            rows = [pl.ds(HELD + w * OWN + part, 8) for w in range(WINS)]
            rec_re = [ready[block, where, :LANES] for where in rows]
            rec_im = [ready[block, where, LANES:] for where in rows]
            rec_sum = [re + im for re, im in zip(rec_re, rec_im)]
            rec_gap = [re - im for re, im in zip(rec_re, rec_im)]
            for index in range(8):
                sums = [None, None, None]
                for w in range(WINS):
                    row = w * 8 + index
                    src_re = jnp.broadcast_to(held[block, row : row + 1, :LANES], (8, LANES))
                    src_im = jnp.broadcast_to(held[block, row : row + 1, LANES:], (8, LANES))
                    src_sum = jnp.broadcast_to(added[block, row : row + 1, :], (8, LANES))
                    terms = (src_sum * rec_re[w], src_im * rec_gap[w], src_re * rec_sum[w])
                    sums = [term if acc is None else acc + term for acc, term in zip(sums, terms)]
                where = pl.ds(index * OWN + part, 8)
                cross[block, where, :LANES] = (sums[0] - sums[1]).astype(BF16)
                cross[block, where, LANES:] = (sums[0] - sums[2]).astype(BF16)
        return carry

    lax.fori_loop(0, BLOCKS, one_block, 0)
    before_inverse()
    lagged = jnp.dot(cross[0], inverse[0], preferred_element_type=F32)
    for block in range(1, BLOCKS):
        lagged += jnp.dot(cross[block], inverse[block], preferred_element_type=F32)
    for index in range(8):
        count = jnp.zeros((OWN, LANES), F32)
        for w in range(WINS):
            row = w * 8 + index
            source = jnp.broadcast_to(flags[row : row + 1, :], (OWN, LANES))
            count += source * rec_flags[w * OWN : w * OWN + OWN, :]
        scale = lax.rsqrt(jnp.maximum(count, 1.0))
        for piece in range(LAGS // LANES):
            lanes = slice(piece * LANES, (piece + 1) * LANES)
            store(index, lanes, (lagged[index * OWN : index * OWN + OWN, lanes] * scale).astype(BF16))


def own_kernel(send, ready, rec_flags, inverse_hbm, own_lags, inverse, held, added, cross, sem):
    inverse_copy = pltpu.make_async_copy(inverse_hbm, inverse, sem)
    inverse_copy.start()

    def store(index, lanes, values):
        own_lags[index, :, lanes] = values

    usable = send[BLOCKS, :, :LANES].astype(F32)
    correlate(send, usable, ready, rec_flags, inverse, store, held, added, cross, inverse_copy.wait)


def other_kernel(received, ready, rec_flags, inverse, own_lags, out_ref, held, added, cross):
    core = lax.axis_index("core")
    out_ref[pl.ds(core * 8, 8)] = own_lags[...]

    def store(index, lanes, values):
        out_ref[(1 - core) * 8 + index, :, lanes] = values

    usable = received[BLOCKS, :, :LANES].astype(F32)
    correlate(received, usable, ready, rec_flags, inverse, store, held, added, cross, lambda: None)


def in_vmem(value):
    return pltpu.with_memory_space_constraint(value, pltpu.VMEM)


def in_hbm(value):
    return pltpu.with_memory_space_constraint(jnp.asarray(value), pltpu.HBM)


def local(records, usable, sources):
    rows_in = records.reshape(OWN, LENGTH)
    slices, rows = pl.pallas_call(
        centre_kernel,
        out_specs=[VMEM_SPEC] * 2,
        out_shape=(pltpu.VMEM((2 * SLICES, OWN, LANES), BF16), pltpu.VMEM((OWN, LENGTH), BF16)),
    )(rows_in, usable.reshape(1, OWN))
    all_channels = lax.all_to_all(slices, ("x", "z", "core"), 0, 0)
    opposite = lax.ppermute(rows, "zh", [(0, 1), (1, 0)])
    picked, pair, token = pl.pallas_call(
        pick_kernel,
        in_specs=[VMEM_SPEC] * 4,
        out_specs=[VMEM_SPEC] * 3,
        out_shape=(
            pltpu.VMEM((SLICES * WINS, 8, LANES), BF16),
            pltpu.VMEM((2 * OWN, LENGTH), BF16),
            pltpu.VMEM((8, LANES), F32),
        ),
    )(sources.reshape(1, SOURCES), in_vmem(all_channels), in_vmem(rows), in_vmem(opposite))
    table = pl.pallas_call(
        load_kernel,
        in_specs=[VMEM_SPEC, HBM_SPEC],
        out_specs=VMEM_SPEC,
        out_shape=pltpu.VMEM((BLOCKS // 2, FOLD, 2 * LANES), BF16),
        scratch_shapes=[pltpu.SemaphoreType.DMA(())],
        compiler_params=pltpu.CompilerParams(vmem_limit_bytes=2**20),
    )(token, in_hbm(forward_table()[: BLOCKS // 2]))
    nexts = [lax.ppermute(pair, "y", [(i, (i + k) % 4) for i in range(4)]) for k in (1, 2, 3)]
    own = lax.all_to_all(picked, ("x", "z", "y", "zh"), 0, 0)
    own, nexts, table = lax.optimization_barrier((own, nexts, table))
    own = own.reshape(SLICES, WINS, 8, LANES)
    rows = HELD + WINS * OWN
    limit = pltpu.CompilerParams(vmem_limit_bytes=16 * 2**20)
    ready, send, flags = pl.pallas_call(
        whiten_kernel,
        in_specs=[VMEM_SPEC] * 6 + [HBM_SPEC],
        out_specs=[VMEM_SPEC] * 3,
        out_shape=(
            pltpu.VMEM((BLOCKS, rows, 2 * LANES), F32),
            pltpu.VMEM((BLOCKS + 1, HELD, 2 * LANES), BF16),
            pltpu.VMEM((WINS * OWN, LANES), F32),
        ),
        scratch_shapes=[
            pltpu.VMEM((BLOCKS // 2, FOLD, 2 * LANES), BF16),
            pltpu.VMEM((rows, FOLD), BF16),
            pltpu.VMEM((rows, FOLD), BF16),
            pltpu.VMEM((rows, BINS), BF16),
            pltpu.SemaphoreType.DMA(()),
        ],
        compiler_params=limit,
    )(
        *(in_vmem(value) for value in (own, pair, *nexts, table)),
        in_hbm(forward_table()[BLOCKS // 2 :]),
    )
    received = lax.ppermute(send, "core", [(0, 1), (1, 0)])
    scratch = [
        pltpu.VMEM((BLOCKS, HELD, 2 * LANES), F32),
        pltpu.VMEM((BLOCKS, HELD, LANES), F32),
        pltpu.VMEM((BLOCKS, 8 * OWN, 2 * LANES), BF16),
    ]
    own_lags, inverse = pl.pallas_call(
        own_kernel,
        in_specs=[VMEM_SPEC] * 3 + [HBM_SPEC],
        out_specs=[VMEM_SPEC] * 2,
        out_shape=(pltpu.VMEM((8, OWN, LAGS), BF16), pltpu.VMEM((BLOCKS, 2 * LANES, LAGS), BF16)),
        scratch_shapes=[*scratch, pltpu.SemaphoreType.DMA(())],
        compiler_params=limit,
    )(*(in_vmem(value) for value in (send, ready, flags)), in_hbm(inverse_table()))
    return pl.pallas_call(
        other_kernel,
        out_shape=jax.ShapeDtypeStruct((OWN, OWN, LAGS), BF16),
        in_specs=[VMEM_SPEC] * 5,
        scratch_shapes=scratch,
        compiler_params=limit,
    )(*(in_vmem(value) for value in (received, ready, flags, inverse, own_lags)))


def solution(mesh):
    split = Mesh(mesh.devices.reshape(4, 4, 2, 4, 2), ("x", "z", "core", "y", "zh"))
    recv, win = ("x", "z", "core"), ("y", "zh")
    in_specs = (P(recv, win, None), P(recv, win), P())
    out_specs = P(win, recv, None)
    return jax.shard_map(local, mesh=split, in_specs=in_specs, out_specs=out_specs, check_vma=False)
```

```python
import functools
import math

import jax
import jax.numpy as jnp
import numpy as np
from jax import lax
from jax.experimental import pallas as pl
from jax.experimental.pallas import tpu as pltpu
from jax.sharding import Mesh
from jax.sharding import PartitionSpec as P

LENGTH = 2048
BINS = LENGTH // 2
FOLD = LENGTH // 2
HALF = 256
LAGS = 2 * HALF
SMOOTH = 32
LANES = 128
SLICES = LENGTH // LANES
BLOCKS = BINS // LANES
WINS = 8
OWN = 16
SOURCES = 128
CHANNELS = 512
HELD = WINS * 8
EARLY = 5
MARK = 1e30
MARK_LIMIT = 1e29
BF16 = jnp.bfloat16
VMEM_SPEC = pl.BlockSpec(memory_space=pltpu.VMEM)
HBM_SPEC = pl.BlockSpec(memory_space=pltpu.HBM)
F32 = jnp.float32


def bin_order():
    lower = np.arange(BINS // 2)
    upper = BINS - lower
    upper[0] = BINS // 2
    return np.concatenate([lower, upper])


def forward_table():
    samples = np.arange(LENGTH).reshape(FOLD, 2).T[:, :, None]
    bins = np.arange(BINS // 2)[None, None, :]

    def angle(product):
        return (product % LENGTH).astype(np.float32) * np.float32(2.0 * math.pi / LENGTH)

    phases = angle(samples * bins)
    real, imag = np.cos(phases), -np.sin(phases)
    middle = angle(samples[:, :, 0] * (BINS // 2))
    imag[0, :, 0] = np.cos(middle[0])
    imag[1, :, 0] = -np.sin(middle[1])
    table = np.stack([real, imag], axis=2).reshape(2, FOLD, 2, BLOCKS // 2, LANES)
    return table.transpose(3, 0, 1, 2, 4).reshape(BLOCKS, FOLD, 2 * LANES).astype(jnp.bfloat16)


def inverse_table():
    bins = bin_order()[:, None]
    lags = np.arange(LAGS)[None, :] - HALF
    phases = (bins * lags % LENGTH).astype(np.float32) * np.float32(2.0 * math.pi / LENGTH)
    factor = np.where(bins == 0, 1.0, 2.0).astype(np.float32) / np.float32(math.sqrt(LENGTH))
    table = np.stack([factor * np.cos(phases), -factor * np.sin(phases)], axis=0)
    table = table.reshape(2, BLOCKS, LANES, LAGS).transpose(1, 0, 2, 3)
    return table.reshape(BLOCKS, 2 * LANES, LAGS).astype(jnp.bfloat16)


def centre_kernel(records_ref, usable_ref, slices_ref, rows_ref):
    widened = records_ref[...].astype(F32)
    mean = jnp.sum(widened, axis=1, keepdims=True) * (1.0 / LENGTH)
    centred = widened - mean
    row_ids = lax.broadcasted_iota(jnp.int32, (OWN, OWN), 0)
    col_ids = lax.broadcasted_iota(jnp.int32, (OWN, OWN), 1)
    flags = jnp.broadcast_to(usable_ref[...].astype(F32), (OWN, OWN))
    flag = jnp.sum(jnp.where(row_ids == col_ids, flags, 0.0), axis=1, keepdims=True)
    marked = jnp.where(flag > 0.5, centred, MARK).astype(BF16)
    wide = 2 * LANES
    from_ids = lax.broadcasted_iota(jnp.int32, (wide, wide), 0)
    to_ids = lax.broadcasted_iota(jnp.int32, (wide, wide), 1)
    taken = jnp.where(to_ids < LANES, 2 * to_ids, 2 * (to_ids - LANES) + 1)
    move = (from_ids == taken).astype(F32).astype(BF16)
    marked = jnp.concatenate(
        [
            jnp.dot(marked[:, p : p + wide], move, preferred_element_type=F32).astype(BF16)
            for p in range(0, LENGTH, wide)
        ],
        axis=1,
    )
    rows_ref[...] = marked
    for part in range(SLICES):
        piece = marked[:, part * LANES : (part + 1) * LANES]
        slices_ref[2 * part] = piece
        slices_ref[2 * part + 1] = piece


def pick_kernel(sources_ref, all_ref, rows_ref, opposite_ref, picked_ref, pair_ref, token_ref):
    pair_ref[:OWN] = rows_ref[...]
    pair_ref[OWN:] = opposite_ref[...]
    core = lax.axis_index("core")
    rows = all_ref[...].reshape(CHANNELS, LANES)
    channel_ids = lax.broadcasted_iota(jnp.int32, (CHANNELS, SOURCES), 0)
    onehot = (channel_ids == sources_ref[...]).astype(F32).astype(BF16)
    picked = lax.dot_general(
        onehot, rows, (((0,), (0,)), ((), ())), preferred_element_type=F32
    ).reshape(WINS, 2, 8, LANES)
    half = jnp.where(core == 0, picked[:, 0], picked[:, 1]).astype(BF16)
    for place in range(SLICES):
        picked_ref[pl.ds(place * WINS, WINS)] = half
    token_ref[...] = jnp.zeros((8, LANES), F32)


def load_kernel(token_ref, table_hbm, table_ref, sem):
    del token_ref
    copy = pltpu.make_async_copy(table_hbm, table_ref, sem)
    copy.start()
    copy.wait()


def unmark(values):
    widened = values.astype(F32)
    return jnp.where(widened > MARK_LIMIT, 0.0, widened).astype(BF16)


def usable_lanes(values):
    return (values.astype(F32) < MARK_LIMIT).astype(F32)


def band_tiles():
    rows = lax.broadcasted_iota(jnp.int32, (2 * LANES, 2 * LANES), 0)
    cols = lax.broadcasted_iota(jnp.int32, (2 * LANES, 2 * LANES), 1)
    low, last = 2 * LANES, 2 * LANES - SMOOTH

    def tile(inside):
        return inside.astype(F32).astype(BF16)

    near = jnp.abs(rows - cols) <= SMOOTH
    below = jnp.abs(rows - cols - low) <= SMOOTH
    above = jnp.abs(rows - cols + low) <= SMOOTH
    row_middle, col_middle = (rows == 0) & (cols >= last), (cols == 0) & (rows >= last)
    alone = (rows == 0) == (cols == 0)
    same = tile(near)
    facing = tile(rows + cols >= 2 * low - SMOOTH)
    return {
        (0, 0): same, (0, 1): tile(below), (1, 0): tile(above), (1, 1): same,
        (2, 2): tile(near & alone), (2, 3): tile(below | row_middle), (3, 2): tile(above | col_middle),
        (3, 3): same, (1, 3): facing, (3, 1): facing, (1, 2): tile(col_middle), (2, 1): tile(row_middle),
    }


def whiten(even, odd, early_table, late_table, late_copies, spec, amp):
    bands = band_tiles()
    lane_ids = lax.broadcasted_iota(jnp.int32, (1, LANES), 1)

    def table(place):
        if place < EARLY:
            return early_table[place]
        late_copies[place - EARLY].wait()
        return late_table[place - EARLY]

    for block in range(BLOCKS // 2):
        evens = jnp.dot(even[...], table(2 * block), preferred_element_type=F32)
        odds = jnp.dot(odd[...], table(2 * block + 1), preferred_element_type=F32)
        lower, upper = evens + odds, evens - odds
        lower_re, lower_im = lower[:, :LANES], lower[:, LANES:]
        upper_re, upper_im = upper[:, :LANES], -upper[:, LANES:]
        if block == 0:
            first = lane_ids == 0
            lower_im = jnp.where(first, 0.0, lower_im)
            upper_re = jnp.where(first, evens[:, LANES:], upper_re)
            upper_im = jnp.where(first, odds[:, LANES:], upper_im)
        for place, real, imag in ((block, lower_re, lower_im), (block + BLOCKS // 2, upper_re, upper_im)):
            spec[place, :, :LANES] = real
            spec[place, :, LANES:] = imag
            amp[:, pl.ds(place * LANES, LANES)] = jnp.sqrt(real * real + imag * imag).astype(BF16)

    wide_ids = lax.broadcasted_iota(jnp.int32, (1, 2 * LANES), 1)
    for pair in range(BLOCKS // 2):
        total = None
        for other in range(BLOCKS // 2):
            if (other, pair) in bands:
                near = jnp.dot(
                    amp[:, pl.ds(other * 2 * LANES, 2 * LANES)],
                    bands[other, pair],
                    preferred_element_type=F32,
                )
                total = near if total is None else total + near
        bin_ids = wide_ids + (pair % 2) * 2 * LANES
        if pair >= 2:
            bin_ids = jnp.where(bin_ids == 0, BINS // 2, BINS - bin_ids)
        count = jnp.minimum(bin_ids, SMOOTH) + jnp.minimum(BINS - 1 - bin_ids, SMOOTH) + 1
        scale = 1.0 / (total * (1.0 / count.astype(F32)) + 1e-6)
        for half in range(2):
            block = 2 * pair + half
            piece = scale[:, half * LANES : (half + 1) * LANES]
            spec[block, :, :LANES] = spec[block, :, :LANES] * piece
            spec[block, :, LANES:] = spec[block, :, LANES:] * piece


def whiten_kernel(
    own_ref, pair_ref, next1_ref, next2_ref, next3_ref, early_table, late_hbm, inverse_hbm,
    spec, send, flags, inverse, late_table, even, odd, amp, sems,
):
    late_copies = [
        pltpu.make_async_copy(late_hbm.at[part], late_table.at[part], sems.at[part])
        for part in range(BLOCKS - EARLY)
    ]
    for copy in late_copies:
        copy.start()
    inverse_copy = pltpu.make_async_copy(inverse_hbm, inverse, sems.at[BLOCKS - EARLY])
    inverse_copy.start()
    line = lax.axis_index("y")
    side = lax.axis_index("zh")
    for part in range(SLICES // 2):
        lanes = pl.ds(part * LANES, LANES)
        even[pl.ds(0, HELD), lanes] = unmark(own_ref[2 * part].reshape(HELD, LANES))
        odd[pl.ds(0, HELD), lanes] = unmark(own_ref[2 * part + 1].reshape(HELD, LANES))
    for step, ref in enumerate((pair_ref, next1_ref, next2_ref, next3_ref)):
        for swap in range(2):
            win = lax.rem(line + step, 4) * 2 + lax.rem(side + swap, 2)
            first = pl.multiple_of(win * OWN, OWN)
            where = pl.ds(HELD + first, OWN)
            received = ref[swap * OWN : swap * OWN + OWN, :]
            for part in range(SLICES // 2):
                lanes, start = pl.ds(part * LANES, LANES), 2 * part * LANES
                even[where, lanes] = unmark(received[:, start : start + LANES])
                odd[where, lanes] = unmark(received[:, start + LANES : start + 2 * LANES])
            flags[pl.ds(first, OWN), :] = usable_lanes(received[:, :LANES])
    whiten(even, odd, early_table, late_table, late_copies, spec, amp)
    send[:BLOCKS] = spec[:, :HELD, :].astype(BF16)
    usable = usable_lanes(own_ref[0].reshape(HELD, LANES)).astype(BF16)
    send[BLOCKS, :, :LANES] = usable
    send[BLOCKS, :, LANES:] = usable
    inverse_copy.wait()


def correlate(sources, flags, ready, rec_flags, inverse, store, held, added, cross):
    held[...] = sources[:BLOCKS].astype(F32)
    added[...] = held[:, :, :LANES] + held[:, :, LANES:]

    def one_block(block, carry):
        for part in range(0, OWN, 8):
            rows = [pl.ds(HELD + w * OWN + part, 8) for w in range(WINS)]
            rec_re = [ready[block, where, :LANES] for where in rows]
            rec_im = [ready[block, where, LANES:] for where in rows]
            rec_sum = [re + im for re, im in zip(rec_re, rec_im)]
            rec_gap = [re - im for re, im in zip(rec_re, rec_im)]
            for index in range(8):
                sums = [None, None, None]
                for w in range(WINS):
                    row = w * 8 + index
                    src_re = jnp.broadcast_to(held[block, row : row + 1, :LANES], (8, LANES))
                    src_im = jnp.broadcast_to(held[block, row : row + 1, LANES:], (8, LANES))
                    src_sum = jnp.broadcast_to(added[block, row : row + 1, :], (8, LANES))
                    terms = (src_sum * rec_re[w], src_im * rec_gap[w], src_re * rec_sum[w])
                    sums = [term if acc is None else acc + term for acc, term in zip(sums, terms)]
                where = pl.ds(index * OWN + part, 8)
                cross[block, where, :LANES] = (sums[0] - sums[1]).astype(BF16)
                cross[block, where, LANES:] = (sums[0] - sums[2]).astype(BF16)
        return carry

    lax.fori_loop(0, BLOCKS, one_block, 0)
    lagged = jnp.dot(cross[0], inverse[0], preferred_element_type=F32)
    for block in range(1, BLOCKS):
        lagged += jnp.dot(cross[block], inverse[block], preferred_element_type=F32)
    for index in range(8):
        count = jnp.zeros((OWN, LANES), F32)
        for w in range(WINS):
            row = w * 8 + index
            source = jnp.broadcast_to(flags[row : row + 1, :], (OWN, LANES))
            count += source * rec_flags[w * OWN : w * OWN + OWN, :]
        scale = lax.rsqrt(jnp.maximum(count, 1.0))
        for piece in range(LAGS // LANES):
            lanes = slice(piece * LANES, (piece + 1) * LANES)
            store(index, lanes, (lagged[index * OWN : index * OWN + OWN, lanes] * scale).astype(BF16))


def own_kernel(send, ready, rec_flags, inverse, own_lags, held, added, cross):
    def store(index, lanes, values):
        own_lags[index, :, lanes] = values

    usable = send[BLOCKS, :, :LANES].astype(F32)
    correlate(send, usable, ready, rec_flags, inverse, store, held, added, cross)


def other_kernel(received, ready, rec_flags, inverse, own_lags, out_ref, held, added, cross):
    core = lax.axis_index("core")
    out_ref[pl.ds(core * 8, 8)] = own_lags[...]

    def store(index, lanes, values):
        out_ref[(1 - core) * 8 + index, :, lanes] = values

    usable = received[BLOCKS, :, :LANES].astype(F32)
    correlate(received, usable, ready, rec_flags, inverse, store, held, added, cross)


def in_vmem(value):
    return pltpu.with_memory_space_constraint(value, pltpu.VMEM)


def in_hbm(value):
    return pltpu.with_memory_space_constraint(jnp.asarray(value), pltpu.HBM)


def local(records, usable, sources):
    rows_in = records.reshape(OWN, LENGTH)
    slices, rows = pl.pallas_call(
        centre_kernel,
        out_specs=[VMEM_SPEC] * 2,
        out_shape=(pltpu.VMEM((2 * SLICES, OWN, LANES), BF16), pltpu.VMEM((OWN, LENGTH), BF16)),
    )(rows_in, usable.reshape(1, OWN))
    all_channels = lax.cond(
        lax.axis_index("core") < 2, lambda v: lax.all_to_all(v, ("x", "z", "core"), 0, 0), lambda v: v, slices
    )
    opposite = lax.ppermute(rows, "zh", [(0, 1), (1, 0)])
    picked, pair, token = pl.pallas_call(
        pick_kernel,
        in_specs=[VMEM_SPEC] * 4,
        out_specs=[VMEM_SPEC] * 3,
        out_shape=(
            pltpu.VMEM((SLICES * WINS, 8, LANES), BF16),
            pltpu.VMEM((2 * OWN, LENGTH), BF16),
            pltpu.VMEM((8, LANES), F32),
        ),
    )(sources.reshape(1, SOURCES), in_vmem(all_channels), in_vmem(rows), in_vmem(opposite))
    table = pl.pallas_call(
        load_kernel,
        in_specs=[VMEM_SPEC, HBM_SPEC],
        out_specs=VMEM_SPEC,
        out_shape=pltpu.VMEM((EARLY, FOLD, 2 * LANES), BF16),
        scratch_shapes=[pltpu.SemaphoreType.DMA(())],
        compiler_params=pltpu.CompilerParams(vmem_limit_bytes=2**20),
    )(token, in_hbm(forward_table()[:EARLY]))
    nexts = [lax.ppermute(pair, "y", [(i, (i - k) % 4) for i in range(4)]) for k in (1, 2, 3)]
    own = lax.all_to_all(picked, ("x", "z", "y", "zh"), 0, 0)
    own, nexts, table = lax.optimization_barrier((own, nexts, table))
    own = own.reshape(SLICES, WINS, 8, LANES)
    rows = HELD + WINS * OWN
    limit = pltpu.CompilerParams(vmem_limit_bytes=16 * 2**20)
    ready, send, flags, inverse = pl.pallas_call(
        whiten_kernel,
        in_specs=[VMEM_SPEC] * 6 + [HBM_SPEC] * 2,
        out_specs=[VMEM_SPEC] * 4,
        out_shape=(
            pltpu.VMEM((BLOCKS, rows, 2 * LANES), F32),
            pltpu.VMEM((BLOCKS + 1, HELD, 2 * LANES), BF16),
            pltpu.VMEM((WINS * OWN, LANES), F32),
            pltpu.VMEM((BLOCKS, 2 * LANES, LAGS), BF16),
        ),
        scratch_shapes=[
            pltpu.VMEM((BLOCKS - EARLY, FOLD, 2 * LANES), BF16),
            pltpu.VMEM((rows, FOLD), BF16),
            pltpu.VMEM((rows, FOLD), BF16),
            pltpu.VMEM((rows, BINS), BF16),
            pltpu.SemaphoreType.DMA((BLOCKS - EARLY + 1,)),
        ],
        compiler_params=limit,
    )(
        *(in_vmem(value) for value in (own, pair, *nexts, table)),
        in_hbm(forward_table()[EARLY:]),
        in_hbm(inverse_table()),
    )
    received = lax.ppermute(send, "core", [(0, 1), (1, 0)])
    scratch = [
        pltpu.VMEM((BLOCKS, HELD, 2 * LANES), F32),
        pltpu.VMEM((BLOCKS, HELD, LANES), F32),
        pltpu.VMEM((BLOCKS, 8 * OWN, 2 * LANES), BF16),
    ]
    own_lags = pl.pallas_call(
        own_kernel,
        in_specs=[VMEM_SPEC] * 4,
        out_specs=VMEM_SPEC,
        out_shape=pltpu.VMEM((8, OWN, LAGS), BF16),
        scratch_shapes=scratch,
        compiler_params=limit,
    )(*(in_vmem(value) for value in (send, ready, flags, inverse)))
    return pl.pallas_call(
        other_kernel,
        out_shape=jax.ShapeDtypeStruct((OWN, OWN, LAGS), BF16),
        in_specs=[VMEM_SPEC] * 5,
        scratch_shapes=scratch,
        compiler_params=limit,
    )(*(in_vmem(value) for value in (received, ready, flags, inverse, own_lags)))


def solution(mesh):
    split = Mesh(mesh.devices.reshape(4, 4, 2, 4, 2), ("x", "z", "core", "y", "zh"))
    recv, win = ("x", "z", "core"), ("y", "zh")
    in_specs = (P(recv, win, None), P(recv, win), P())
    out_specs = P(win, recv, None)
    return jax.shard_map(local, mesh=split, in_specs=in_specs, out_specs=out_specs, check_vma=False)
```

```python
import functools
import math

import jax
import jax.numpy as jnp
import numpy as np
from jax import lax
from jax.experimental import pallas as pl
from jax.experimental.pallas import tpu as pltpu
from jax.sharding import Mesh
from jax.sharding import PartitionSpec as P

LENGTH = 2048
BINS = LENGTH // 2
HALF = 256
LAGS = 2 * HALF
SMOOTH = 32
LANES = 128
SLICES = LENGTH // LANES
BLOCKS = BINS // LANES
WINS = 8
OWN = 16
SOURCES = 128
CHANNELS = 512
HELD = WINS * 8
EIGHTH = 0.70703125
MARK = 1e30
MARK_LIMIT = 1e29
BF16 = jnp.bfloat16
VMEM_SPEC = pl.BlockSpec(memory_space=pltpu.VMEM)
HBM_SPEC = pl.BlockSpec(memory_space=pltpu.HBM)
F32 = jnp.float32


def bin_order():
    low = np.arange(BINS // 4)
    order = np.stack([low, BINS // 2 - low, BINS // 2 + low, BINS - low])
    order[1, 0], order[3, 0] = BINS // 4, 3 * BINS // 4
    return order.reshape(-1)


def forward_table():
    samples = np.arange(LENGTH).reshape(LENGTH // 4, 4).T[:, :, None]
    bins = np.arange(BINS // 4)[None, None, :]
    phases = (samples * bins % LENGTH).astype(np.float32) * np.float32(2.0 * math.pi / LENGTH)
    real, imag = np.cos(phases), -np.sin(phases)
    imag[:, :, 0] = 1 - 2 * (np.arange(LENGTH // 4) % 2)
    table = np.stack([real, imag], axis=2).reshape(4, LENGTH // 4, 2, 2, LANES)
    return table.transpose(3, 0, 1, 2, 4).reshape(8, LENGTH // 4, 2 * LANES).astype(jnp.bfloat16)


def inverse_table():
    bins = bin_order()[:, None]
    lags = np.arange(LAGS)[None, :] - HALF
    phases = (bins * lags % LENGTH).astype(np.float32) * np.float32(2.0 * math.pi / LENGTH)
    factor = np.where(bins == 0, 1.0, 2.0).astype(np.float32) / np.float32(math.sqrt(LENGTH))
    table = np.stack([factor * np.cos(phases), -factor * np.sin(phases)], axis=0)
    table = table.reshape(2, BLOCKS, LANES, LAGS).transpose(1, 0, 2, 3)
    return table.reshape(BLOCKS, 2 * LANES, LAGS).astype(jnp.bfloat16)


def centre_kernel(records_ref, usable_ref, slices_ref, rows_ref):
    widened = records_ref[...].astype(F32)
    mean = jnp.sum(widened, axis=1, keepdims=True) * (1.0 / LENGTH)
    centred = widened - mean
    row_ids = lax.broadcasted_iota(jnp.int32, (OWN, OWN), 0)
    col_ids = lax.broadcasted_iota(jnp.int32, (OWN, OWN), 1)
    flags = jnp.broadcast_to(usable_ref[...].astype(F32), (OWN, OWN))
    flag = jnp.sum(jnp.where(row_ids == col_ids, flags, 0.0), axis=1, keepdims=True)
    marked = jnp.where(flag > 0.5, centred, MARK).astype(BF16)
    wide = 4 * LANES
    from_ids = lax.broadcasted_iota(jnp.int32, (wide, wide), 0)
    to_ids = lax.broadcasted_iota(jnp.int32, (wide, wide), 1)
    taken = 4 * lax.rem(to_ids, LANES) + lax.div(to_ids, LANES)
    move = (from_ids == taken).astype(F32).astype(BF16)
    marked = jnp.concatenate(
        [
            jnp.dot(marked[:, p : p + wide], move, preferred_element_type=F32).astype(BF16)
            for p in range(0, LENGTH, wide)
        ],
        axis=1,
    )
    rows_ref[...] = marked
    for part in range(SLICES):
        piece = marked[:, part * LANES : (part + 1) * LANES]
        slices_ref[2 * part] = piece
        slices_ref[2 * part + 1] = piece


def pick_kernel(sources_ref, all_ref, rows_ref, opposite_ref, picked_ref, pair_ref, token_ref):
    pair_ref[:OWN] = rows_ref[...]
    pair_ref[OWN:] = opposite_ref[...]
    core = lax.axis_index("core")
    rows = all_ref[...].reshape(CHANNELS, LANES)
    channel_ids = lax.broadcasted_iota(jnp.int32, (CHANNELS, SOURCES), 0)
    onehot = (channel_ids == sources_ref[...]).astype(F32).astype(BF16)
    picked = lax.dot_general(
        onehot, rows, (((0,), (0,)), ((), ())), preferred_element_type=F32
    ).reshape(WINS, 2, 8, LANES)
    half = jnp.where(core == 0, picked[:, 0], picked[:, 1]).astype(BF16)
    for place in range(SLICES):
        picked_ref[pl.ds(place * WINS, WINS)] = half
    token_ref[...] = jnp.zeros((8, LANES), F32)


def load_kernel(token_ref, table_hbm, table_ref, sem):
    del token_ref
    copy = pltpu.make_async_copy(table_hbm, table_ref, sem)
    copy.start()
    copy.wait()


def unmark(values):
    widened = values.astype(F32)
    return jnp.where(widened > MARK_LIMIT, 0.0, widened).astype(BF16)


def usable_lanes(values):
    return (values.astype(F32) < MARK_LIMIT).astype(F32)


def bins_of(group, slot):
    if group % 2 == 0:
        return slot + group * (BINS // 4)
    return jnp.where(slot == 0, group * (BINS // 4), (group + 1) * (BINS // 4) - slot)


def band_tiles():
    rows = lax.broadcasted_iota(jnp.int32, (2 * LANES, 2 * LANES), 0)
    cols = lax.broadcasted_iota(jnp.int32, (2 * LANES, 2 * LANES), 1)
    tiles = {}
    for pair in ((0, 0), (1, 1), (0, 1), (1, 0), (1, 2), (2, 1)):
        apart = jnp.abs(bins_of(pair[0], rows) - bins_of(pair[1], cols))
        tiles[pair] = (apart <= SMOOTH).astype(F32).astype(BF16)
    for pair in ((2, 2), (3, 3), (2, 3), (3, 2)):
        tiles[pair] = tiles[pair[0] - 2, pair[1] - 2]
    return tiles


def whiten(classes, table, spec, amp):
    bands = band_tiles()
    first = lax.broadcasted_iota(jnp.int32, (1, LANES), 1) == 0
    for block in range(2):
        parts = [jnp.dot(classes[r], table[4 * block + r], preferred_element_type=F32) for r in range(4)]
        real = [part[:, :LANES] for part in parts]
        imag = [part[:, LANES:] for part in parts]
        sum02_re, sum02_im, gap02_re, gap02_im = real[0] + real[2], imag[0] + imag[2], real[0] - real[2], imag[0] - imag[2]
        sum13_re, sum13_im, gap13_re, gap13_im = real[1] + real[3], imag[1] + imag[3], real[1] - real[3], imag[1] - imag[3]
        bins = [
            (sum02_re + sum13_re, sum02_im + sum13_im),
            (gap02_re - gap13_im, -gap02_im - gap13_re),
            (gap02_re + gap13_im, gap02_im - gap13_re),
            (sum02_re - sum13_re, sum13_im - sum02_im),
        ]
        if block == 0:
            gap, both = EIGHTH * gap13_im, EIGHTH * sum13_im
            special = [
                (bins[0][0], jnp.zeros_like(gap)),
                (imag[0] + gap, -imag[2] - both),
                (gap02_re, -gap13_re),
                (imag[0] - gap, imag[2] - both),
            ]
            bins = [
                tuple(jnp.where(first, new, old) for new, old in zip(at_first, at_rest))
                for at_first, at_rest in zip(special, bins)
            ]
        for group, (re, im) in enumerate(bins):
            place = 2 * group + block
            spec[place, :, :LANES] = re
            spec[place, :, LANES:] = im
            amp[:, pl.ds(place * LANES, LANES)] = jnp.sqrt(re * re + im * im).astype(BF16)

    wide_ids = lax.broadcasted_iota(jnp.int32, (1, 2 * LANES), 1)
    for group in range(4):
        total = None
        for other in range(4):
            if (other, group) in bands:
                near = jnp.dot(
                    amp[:, pl.ds(other * 2 * LANES, 2 * LANES)],
                    bands[other, group],
                    preferred_element_type=F32,
                )
                total = near if total is None else total + near
        bin_ids = bins_of(group, wide_ids)
        count = jnp.minimum(bin_ids, SMOOTH) + jnp.minimum(BINS - 1 - bin_ids, SMOOTH) + 1
        scale = 1.0 / (total * (1.0 / count.astype(F32)) + 1e-6)
        for half in range(2):
            block = 2 * group + half
            piece = scale[:, half * LANES : (half + 1) * LANES]
            spec[block, :, :LANES] = spec[block, :, :LANES] * piece
            spec[block, :, LANES:] = spec[block, :, LANES:] * piece


def whiten_kernel(
    own_ref, pair_ref, next1_ref, next2_ref, next3_ref, table, inverse_hbm,
    spec, send, flags, inverse, classes, amp, sem,
):
    inverse_copy = pltpu.make_async_copy(inverse_hbm, inverse, sem)
    inverse_copy.start()
    line = lax.axis_index("y")
    side = lax.axis_index("zh")
    for part in range(SLICES):
        lanes = pl.ds(part // 4 * LANES, LANES)
        classes[part % 4, pl.ds(0, HELD), lanes] = unmark(own_ref[part].reshape(HELD, LANES))
    for step, ref in enumerate((pair_ref, next1_ref, next2_ref, next3_ref)):
        for swap in range(2):
            win = lax.rem(line + step, 4) * 2 + lax.rem(side + swap, 2)
            first = pl.multiple_of(win * OWN, OWN)
            where = pl.ds(HELD + first, OWN)
            received = ref[swap * OWN : swap * OWN + OWN, :]
            for part in range(SLICES):
                lanes = pl.ds(part // 4 * LANES, LANES)
                classes[part % 4, where, lanes] = unmark(received[:, part * LANES : (part + 1) * LANES])
            flags[pl.ds(first, OWN), :] = usable_lanes(received[:, :LANES])
    whiten(classes, table, spec, amp)
    send[:BLOCKS] = spec[:, :HELD, :].astype(BF16)
    usable = usable_lanes(own_ref[0].reshape(HELD, LANES)).astype(BF16)
    send[BLOCKS, :, :LANES] = usable
    send[BLOCKS, :, LANES:] = usable
    inverse_copy.wait()


def correlate(sources, flags, ready, rec_flags, inverse, store, held, added, cross):
    held[...] = sources[:BLOCKS].astype(F32)
    added[...] = held[:, :, :LANES] + held[:, :, LANES:]

    def one_block(block, carry):
        for part in range(0, OWN, 8):
            rows = [pl.ds(HELD + w * OWN + part, 8) for w in range(WINS)]
            rec_re = [ready[block, where, :LANES] for where in rows]
            rec_im = [ready[block, where, LANES:] for where in rows]
            rec_sum = [re + im for re, im in zip(rec_re, rec_im)]
            rec_gap = [re - im for re, im in zip(rec_re, rec_im)]
            for index in range(8):
                sums = [None, None, None]
                for w in range(WINS):
                    row = w * 8 + index
                    src_re = jnp.broadcast_to(held[block, row : row + 1, :LANES], (8, LANES))
                    src_im = jnp.broadcast_to(held[block, row : row + 1, LANES:], (8, LANES))
                    src_sum = jnp.broadcast_to(added[block, row : row + 1, :], (8, LANES))
                    terms = (src_sum * rec_re[w], src_im * rec_gap[w], src_re * rec_sum[w])
                    sums = [term if acc is None else acc + term for acc, term in zip(sums, terms)]
                where = pl.ds(index * OWN + part, 8)
                cross[block, where, :LANES] = (sums[0] - sums[1]).astype(BF16)
                cross[block, where, LANES:] = (sums[0] - sums[2]).astype(BF16)
        return carry

    lax.fori_loop(0, BLOCKS, one_block, 0)
    lagged = jnp.dot(cross[0], inverse[0], preferred_element_type=F32)
    for block in range(1, BLOCKS):
        lagged += jnp.dot(cross[block], inverse[block], preferred_element_type=F32)
    for index in range(8):
        count = jnp.zeros((OWN, LANES), F32)
        for w in range(WINS):
            row = w * 8 + index
            source = jnp.broadcast_to(flags[row : row + 1, :], (OWN, LANES))
            count += source * rec_flags[w * OWN : w * OWN + OWN, :]
        scale = lax.rsqrt(jnp.maximum(count, 1.0))
        for piece in range(LAGS // LANES):
            lanes = slice(piece * LANES, (piece + 1) * LANES)
            store(index, lanes, (lagged[index * OWN : index * OWN + OWN, lanes] * scale).astype(BF16))


def own_kernel(send, ready, rec_flags, inverse, own_lags, held, added, cross):
    def store(index, lanes, values):
        own_lags[index, :, lanes] = values

    usable = send[BLOCKS, :, :LANES].astype(F32)
    correlate(send, usable, ready, rec_flags, inverse, store, held, added, cross)


def other_kernel(received, ready, rec_flags, inverse, own_lags, out_ref, held, added, cross):
    core = lax.axis_index("core")
    out_ref[pl.ds(core * 8, 8)] = own_lags[...]

    def store(index, lanes, values):
        out_ref[(1 - core) * 8 + index, :, lanes] = values

    usable = received[BLOCKS, :, :LANES].astype(F32)
    correlate(received, usable, ready, rec_flags, inverse, store, held, added, cross)


def in_vmem(value):
    return pltpu.with_memory_space_constraint(value, pltpu.VMEM)


def in_hbm(value):
    return pltpu.with_memory_space_constraint(jnp.asarray(value), pltpu.HBM)


def local(records, usable, sources):
    rows_in = records.reshape(OWN, LENGTH)
    slices, rows = pl.pallas_call(
        centre_kernel,
        out_specs=[VMEM_SPEC] * 2,
        out_shape=(pltpu.VMEM((2 * SLICES, OWN, LANES), BF16), pltpu.VMEM((OWN, LENGTH), BF16)),
    )(rows_in, usable.reshape(1, OWN))
    all_channels = lax.cond(
        lax.axis_index("core") < 2, lambda v: lax.all_to_all(v, ("x", "z", "core"), 0, 0), lambda v: v, slices
    )
    opposite = lax.ppermute(rows, "zh", [(0, 1), (1, 0)])
    picked, pair, token = pl.pallas_call(
        pick_kernel,
        in_specs=[VMEM_SPEC] * 4,
        out_specs=[VMEM_SPEC] * 3,
        out_shape=(
            pltpu.VMEM((SLICES * WINS, 8, LANES), BF16),
            pltpu.VMEM((2 * OWN, LENGTH), BF16),
            pltpu.VMEM((8, LANES), F32),
        ),
    )(sources.reshape(1, SOURCES), in_vmem(all_channels), in_vmem(rows), in_vmem(opposite))
    table = pl.pallas_call(
        load_kernel,
        in_specs=[VMEM_SPEC, HBM_SPEC],
        out_specs=VMEM_SPEC,
        out_shape=pltpu.VMEM((8, LENGTH // 4, 2 * LANES), BF16),
        scratch_shapes=[pltpu.SemaphoreType.DMA(())],
        compiler_params=pltpu.CompilerParams(vmem_limit_bytes=2**20),
    )(token, in_hbm(forward_table()))
    nexts = [lax.ppermute(pair, "y", [(i, (i - k) % 4) for i in range(4)]) for k in (1, 2, 3)]
    own = lax.all_to_all(picked, ("x", "z", "y", "zh"), 0, 0)
    own, nexts, table = lax.optimization_barrier((own, nexts, table))
    own = own.reshape(SLICES, WINS, 8, LANES)
    rows = HELD + WINS * OWN
    limit = pltpu.CompilerParams(vmem_limit_bytes=16 * 2**20)
    ready, send, flags, inverse = pl.pallas_call(
        whiten_kernel,
        in_specs=[VMEM_SPEC] * 6 + [HBM_SPEC],
        out_specs=[VMEM_SPEC] * 4,
        out_shape=(
            pltpu.VMEM((BLOCKS, rows, 2 * LANES), F32),
            pltpu.VMEM((BLOCKS + 1, HELD, 2 * LANES), BF16),
            pltpu.VMEM((WINS * OWN, LANES), F32),
            pltpu.VMEM((BLOCKS, 2 * LANES, LAGS), BF16),
        ),
        scratch_shapes=[
            pltpu.VMEM((4, rows, LENGTH // 4), BF16),
            pltpu.VMEM((rows, BINS), BF16),
            pltpu.SemaphoreType.DMA(()),
        ],
        compiler_params=limit,
    )(
        *(in_vmem(value) for value in (own, pair, *nexts, table)),
        in_hbm(inverse_table()),
    )
    received = lax.ppermute(send, "core", [(0, 1), (1, 0)])
    scratch = [
        pltpu.VMEM((BLOCKS, HELD, 2 * LANES), F32),
        pltpu.VMEM((BLOCKS, HELD, LANES), F32),
        pltpu.VMEM((BLOCKS, 8 * OWN, 2 * LANES), BF16),
    ]
    own_lags = pl.pallas_call(
        own_kernel,
        in_specs=[VMEM_SPEC] * 4,
        out_specs=VMEM_SPEC,
        out_shape=pltpu.VMEM((8, OWN, LAGS), BF16),
        scratch_shapes=scratch,
        compiler_params=limit,
    )(*(in_vmem(value) for value in (send, ready, flags, inverse)))
    return pl.pallas_call(
        other_kernel,
        out_shape=jax.ShapeDtypeStruct((OWN, OWN, LAGS), BF16),
        in_specs=[VMEM_SPEC] * 5,
        scratch_shapes=scratch,
        compiler_params=limit,
    )(*(in_vmem(value) for value in (received, ready, flags, inverse, own_lags)))


def solution(mesh):
    split = Mesh(mesh.devices.reshape(4, 4, 2, 4, 2), ("x", "z", "core", "y", "zh"))
    recv, win = ("x", "z", "core"), ("y", "zh")
    in_specs = (P(recv, win, None), P(recv, win), P())
    out_specs = P(win, recv, None)
    return jax.shard_map(local, mesh=split, in_specs=in_specs, out_specs=out_specs, check_vma=False)
```

```python
import functools
import math

import jax
import jax.numpy as jnp
import numpy as np
from jax import lax
from jax.experimental import pallas as pl
from jax.experimental.pallas import tpu as pltpu
from jax.sharding import Mesh
from jax.sharding import PartitionSpec as P

LENGTH = 2048
BINS = LENGTH // 2
HALF = 256
LAGS = 2 * HALF
SMOOTH = 32
LANES = 128
SLICES = LENGTH // LANES
BLOCKS = BINS // LANES
WINS = 8
OWN = 16
SOURCES = 128
CHANNELS = 512
HELD = WINS * 8
EIGHTH = 0.70703125
MARK = 1e30
MARK_LIMIT = 1e29
BF16 = jnp.bfloat16
VMEM_SPEC = pl.BlockSpec(memory_space=pltpu.VMEM)
HBM_SPEC = pl.BlockSpec(memory_space=pltpu.HBM)
F32 = jnp.float32


def bin_order():
    low = np.arange(BINS // 4)
    order = np.stack([low, BINS // 2 - low, BINS // 2 + low, BINS - low])
    order[1, 0], order[3, 0] = BINS // 4, 3 * BINS // 4
    return order.reshape(-1)


def forward_table():
    samples = np.arange(LENGTH).reshape(LENGTH // 4, 4).T[:, :, None]
    bins = np.arange(BINS // 4)[None, None, :]
    phases = (samples * bins % LENGTH).astype(np.float32) * np.float32(2.0 * math.pi / LENGTH)
    real, imag = np.cos(phases), -np.sin(phases)
    imag[:, :, 0] = 1 - 2 * (np.arange(LENGTH // 4) % 2)
    table = np.stack([real, imag], axis=2).reshape(4, LENGTH // 4, 2, 2, LANES)
    return table.transpose(3, 0, 1, 2, 4).reshape(8, LENGTH // 4, 2 * LANES).astype(jnp.bfloat16)


def inverse_table():
    bins = bin_order()[:, None]
    lags = np.arange(LAGS)[None, :] - HALF
    phases = (bins * lags % LENGTH).astype(np.float32) * np.float32(2.0 * math.pi / LENGTH)
    factor = np.where(bins == 0, 1.0, 2.0).astype(np.float32) / np.float32(math.sqrt(LENGTH))
    table = np.stack([factor * np.cos(phases), -factor * np.sin(phases)], axis=0)
    table = table.reshape(2, BLOCKS, LANES, LAGS).transpose(1, 0, 2, 3)
    return table.reshape(BLOCKS, 2 * LANES, LAGS).astype(jnp.bfloat16)


def centre_kernel(records_ref, usable_ref, slices_ref, rows_ref):
    widened = records_ref[...].astype(F32)
    mean = jnp.sum(widened, axis=1, keepdims=True) * (1.0 / LENGTH)
    centred = widened - mean
    row_ids = lax.broadcasted_iota(jnp.int32, (OWN, OWN), 0)
    col_ids = lax.broadcasted_iota(jnp.int32, (OWN, OWN), 1)
    flags = jnp.broadcast_to(usable_ref[...].astype(F32), (OWN, OWN))
    flag = jnp.sum(jnp.where(row_ids == col_ids, flags, 0.0), axis=1, keepdims=True)
    marked = jnp.where(flag > 0.5, centred, MARK).astype(BF16)
    wide = 4 * LANES
    from_ids = lax.broadcasted_iota(jnp.int32, (wide, wide), 0)
    to_ids = lax.broadcasted_iota(jnp.int32, (wide, wide), 1)
    taken = 4 * lax.rem(to_ids, LANES) + lax.div(to_ids, LANES)
    move = (from_ids == taken).astype(F32).astype(BF16)
    marked = jnp.concatenate(
        [
            jnp.dot(marked[:, p : p + wide], move, preferred_element_type=F32).astype(BF16)
            for p in range(0, LENGTH, wide)
        ],
        axis=1,
    )
    rows_ref[...] = marked
    for part in range(SLICES):
        piece = marked[:, part * LANES : (part + 1) * LANES]
        slices_ref[2 * part] = piece
        slices_ref[2 * part + 1] = piece


def pick_kernel(sources_ref, all_ref, rows_ref, opposite_ref, picked_ref, pair_ref, token_ref):
    pair_ref[:OWN] = rows_ref[...]
    pair_ref[OWN:] = opposite_ref[...]
    core = lax.axis_index("core")
    rows = all_ref[...].reshape(CHANNELS, LANES)
    row_ids = lax.broadcasted_iota(jnp.int32, (HELD, SOURCES), 0)
    source_ids = lax.broadcasted_iota(jnp.int32, (HELD, SOURCES), 1)
    here = source_ids == lax.div(row_ids, 8) * 16 + core * 8 + lax.rem(row_ids, 8)
    wanted = jnp.sum(jnp.where(here, sources_ref[...].astype(F32), 0.0), axis=1, keepdims=True)
    channel_ids = lax.broadcasted_iota(jnp.int32, (HELD, CHANNELS), 1)
    onehot = (channel_ids == wanted.astype(jnp.int32)).astype(F32).astype(BF16)
    half = jnp.dot(onehot, rows, preferred_element_type=F32).astype(BF16).reshape(WINS, 8, LANES)
    for place in range(SLICES):
        picked_ref[pl.ds(place * WINS, WINS)] = half
    token_ref[...] = jnp.zeros((8, LANES), F32)


def bins_of(group, slot):
    if group % 2 == 0:
        return slot + group * (BINS // 4)
    return jnp.where(slot == 0, group * (BINS // 4), (group + 1) * (BINS // 4) - slot)


BANDS = ((0, 0), (1, 1), (0, 1), (1, 0), (1, 2))
REPEATS = ((2, 2), (3, 3), (2, 3), (3, 2))


def band_tile(pair):
    rows = lax.broadcasted_iota(jnp.int32, (2 * LANES, 2 * LANES), 0)
    cols = lax.broadcasted_iota(jnp.int32, (2 * LANES, 2 * LANES), 1)
    apart = jnp.abs(bins_of(pair[0], rows) - bins_of(pair[1], cols))
    return (apart <= SMOOTH).astype(F32).astype(BF16)


def load_kernel(token_ref, table_hbm, table_ref, bands_ref, sem):
    del token_ref
    copy = pltpu.make_async_copy(table_hbm, table_ref, sem)
    copy.start()
    for place, pair in enumerate(BANDS):
        bands_ref[place] = band_tile(pair)
    copy.wait()


def unmark(values):
    widened = values.astype(F32)
    return jnp.where(widened > MARK_LIMIT, 0.0, widened).astype(BF16)


def usable_lanes(values):
    return (values.astype(F32) < MARK_LIMIT).astype(F32)


def whiten(classes, table, bands, spec, amp):
    first = lax.broadcasted_iota(jnp.int32, (1, LANES), 1) == 0
    for block in range(2):
        parts = [jnp.dot(classes[r], table[4 * block + r], preferred_element_type=F32) for r in range(4)]
        real = [part[:, :LANES] for part in parts]
        imag = [part[:, LANES:] for part in parts]
        sum02_re, sum02_im, gap02_re, gap02_im = real[0] + real[2], imag[0] + imag[2], real[0] - real[2], imag[0] - imag[2]
        sum13_re, sum13_im, gap13_re, gap13_im = real[1] + real[3], imag[1] + imag[3], real[1] - real[3], imag[1] - imag[3]
        bins = [
            (sum02_re + sum13_re, sum02_im + sum13_im),
            (gap02_re - gap13_im, -gap02_im - gap13_re),
            (gap02_re + gap13_im, gap02_im - gap13_re),
            (sum02_re - sum13_re, sum13_im - sum02_im),
        ]
        if block == 0:
            gap, both = EIGHTH * gap13_im, EIGHTH * sum13_im
            special = [
                (bins[0][0], jnp.zeros_like(gap)),
                (imag[0] + gap, -imag[2] - both),
                (gap02_re, -gap13_re),
                (imag[0] - gap, imag[2] - both),
            ]
            bins = [
                tuple(jnp.where(first, new, old) for new, old in zip(at_first, at_rest))
                for at_first, at_rest in zip(special, bins)
            ]
        for group, (re, im) in enumerate(bins):
            place = 2 * group + block
            spec[place, :, :LANES] = re
            spec[place, :, LANES:] = im
            amp[:, pl.ds(place * LANES, LANES)] = jnp.sqrt(re * re + im * im).astype(BF16)

    tiles = {pair: bands[place] for place, pair in enumerate(BANDS)}
    tiles.update({pair: bands[place] for place, pair in enumerate(REPEATS)})
    tiles[2, 1] = band_tile((2, 1))
    wide_ids = lax.broadcasted_iota(jnp.int32, (1, 2 * LANES), 1)
    for group in range(4):
        total = None
        for other in range(4):
            if (other, group) in tiles:
                near = jnp.dot(
                    amp[:, pl.ds(other * 2 * LANES, 2 * LANES)],
                    tiles[other, group],
                    preferred_element_type=F32,
                )
                total = near if total is None else total + near
        bin_ids = bins_of(group, wide_ids)
        count = jnp.minimum(bin_ids, SMOOTH) + jnp.minimum(BINS - 1 - bin_ids, SMOOTH) + 1
        scale = 1.0 / (total * (1.0 / count.astype(F32)) + 1e-6)
        for half in range(2):
            block = 2 * group + half
            piece = scale[:, half * LANES : (half + 1) * LANES]
            spec[block, :, :LANES] = spec[block, :, :LANES] * piece
            spec[block, :, LANES:] = spec[block, :, LANES:] * piece


def whiten_kernel(
    own_ref, pair_ref, next1_ref, next2_ref, next3_ref, table, bands, inverse_hbm,
    spec, send, flags, inverse, classes, amp, sem,
):
    inverse_copy = pltpu.make_async_copy(inverse_hbm, inverse, sem)
    inverse_copy.start()
    line = lax.axis_index("y")
    side = lax.axis_index("zh")
    for part in range(SLICES):
        lanes = pl.ds(part // 4 * LANES, LANES)
        classes[part % 4, pl.ds(0, HELD), lanes] = unmark(own_ref[part].reshape(HELD, LANES))
    for step, ref in enumerate((pair_ref, next1_ref, next2_ref, next3_ref)):
        for swap in range(2):
            win = lax.rem(line + step, 4) * 2 + lax.rem(side + swap, 2)
            first = pl.multiple_of(win * OWN, OWN)
            where = pl.ds(HELD + first, OWN)
            received = ref[swap * OWN : swap * OWN + OWN, :]
            for part in range(SLICES):
                lanes = pl.ds(part // 4 * LANES, LANES)
                classes[part % 4, where, lanes] = unmark(received[:, part * LANES : (part + 1) * LANES])
            flags[pl.ds(first, OWN), :] = usable_lanes(received[:, :LANES])
    whiten(classes, table, bands, spec, amp)
    send[:BLOCKS] = spec[:, :HELD, :].astype(BF16)
    usable = usable_lanes(own_ref[0].reshape(HELD, LANES)).astype(BF16)
    send[BLOCKS, :, :LANES] = usable
    send[BLOCKS, :, LANES:] = usable
    inverse_copy.wait()


def correlate(sources, flags, ready, rec_flags, inverse, store, held, added, cross):
    held[...] = sources[:BLOCKS].astype(F32)
    added[...] = held[:, :, :LANES] + held[:, :, LANES:]

    def one_block(block, carry):
        for part in range(0, OWN, 8):
            rows = [pl.ds(HELD + w * OWN + part, 8) for w in range(WINS)]
            rec_re = [ready[block, where, :LANES] for where in rows]
            rec_im = [ready[block, where, LANES:] for where in rows]
            rec_sum = [re + im for re, im in zip(rec_re, rec_im)]
            rec_gap = [re - im for re, im in zip(rec_re, rec_im)]
            for index in range(8):
                sums = [None, None, None]
                for w in range(WINS):
                    row = w * 8 + index
                    src_re = jnp.broadcast_to(held[block, row : row + 1, :LANES], (8, LANES))
                    src_im = jnp.broadcast_to(held[block, row : row + 1, LANES:], (8, LANES))
                    src_sum = jnp.broadcast_to(added[block, row : row + 1, :], (8, LANES))
                    terms = (src_sum * rec_re[w], src_im * rec_gap[w], src_re * rec_sum[w])
                    sums = [term if acc is None else acc + term for acc, term in zip(sums, terms)]
                where = pl.ds(index * OWN + part, 8)
                cross[block, where, :LANES] = (sums[0] - sums[1]).astype(BF16)
                cross[block, where, LANES:] = (sums[0] - sums[2]).astype(BF16)
        return carry

    lax.fori_loop(0, BLOCKS, one_block, 0)
    lagged = jnp.dot(cross[0], inverse[0], preferred_element_type=F32)
    for block in range(1, BLOCKS):
        lagged += jnp.dot(cross[block], inverse[block], preferred_element_type=F32)
    for index in range(8):
        count = jnp.zeros((OWN, LANES), F32)
        for w in range(WINS):
            row = w * 8 + index
            source = jnp.broadcast_to(flags[row : row + 1, :], (OWN, LANES))
            count += source * rec_flags[w * OWN : w * OWN + OWN, :]
        scale = lax.rsqrt(jnp.maximum(count, 1.0))
        for piece in range(LAGS // LANES):
            lanes = slice(piece * LANES, (piece + 1) * LANES)
            store(index, lanes, (lagged[index * OWN : index * OWN + OWN, lanes] * scale).astype(BF16))


def own_kernel(send, ready, rec_flags, inverse, own_lags, held, added, cross):
    def store(index, lanes, values):
        own_lags[index, :, lanes] = values

    usable = send[BLOCKS, :, :LANES].astype(F32)
    correlate(send, usable, ready, rec_flags, inverse, store, held, added, cross)


def other_kernel(received, ready, rec_flags, inverse, own_lags, out_ref, held, added, cross):
    core = lax.axis_index("core")
    out_ref[pl.ds(core * 8, 8)] = own_lags[...]

    def store(index, lanes, values):
        out_ref[(1 - core) * 8 + index, :, lanes] = values

    usable = received[BLOCKS, :, :LANES].astype(F32)
    correlate(received, usable, ready, rec_flags, inverse, store, held, added, cross)


def in_vmem(value):
    return pltpu.with_memory_space_constraint(value, pltpu.VMEM)


def in_hbm(value):
    return pltpu.with_memory_space_constraint(jnp.asarray(value), pltpu.HBM)


def local(records, usable, sources):
    rows_in = records.reshape(OWN, LENGTH)
    slices, rows = pl.pallas_call(
        centre_kernel,
        out_specs=[VMEM_SPEC] * 2,
        out_shape=(pltpu.VMEM((2 * SLICES, OWN, LANES), BF16), pltpu.VMEM((OWN, LENGTH), BF16)),
    )(rows_in, usable.reshape(1, OWN))
    all_channels = lax.cond(
        lax.axis_index("core") < 2, lambda v: lax.all_to_all(v, ("x", "z", "core"), 0, 0), lambda v: v, slices
    )
    opposite = lax.ppermute(rows, "zh", [(0, 1), (1, 0)])
    picked, pair, token = pl.pallas_call(
        pick_kernel,
        in_specs=[VMEM_SPEC] * 4,
        out_specs=[VMEM_SPEC] * 3,
        out_shape=(
            pltpu.VMEM((SLICES * WINS, 8, LANES), BF16),
            pltpu.VMEM((2 * OWN, LENGTH), BF16),
            pltpu.VMEM((8, LANES), F32),
        ),
    )(sources.reshape(1, SOURCES), in_vmem(all_channels), in_vmem(rows), in_vmem(opposite))
    table, bands = pl.pallas_call(
        load_kernel,
        in_specs=[VMEM_SPEC, HBM_SPEC],
        out_specs=[VMEM_SPEC] * 2,
        out_shape=(
            pltpu.VMEM((8, LENGTH // 4, 2 * LANES), BF16),
            pltpu.VMEM((5, 2 * LANES, 2 * LANES), BF16),
        ),
        scratch_shapes=[pltpu.SemaphoreType.DMA(())],
        compiler_params=pltpu.CompilerParams(vmem_limit_bytes=2**20),
    )(token, in_hbm(forward_table()))
    nexts = [lax.ppermute(pair, "y", [(i, (i - k) % 4) for i in range(4)]) for k in (1, 2, 3)]
    own = lax.all_to_all(picked, ("x", "z", "y", "zh"), 0, 0)
    own, nexts, table, bands = lax.optimization_barrier((own, nexts, table, bands))
    own = own.reshape(SLICES, WINS, 8, LANES)
    rows = HELD + WINS * OWN
    limit = pltpu.CompilerParams(vmem_limit_bytes=16 * 2**20)
    ready, send, flags, inverse = pl.pallas_call(
        whiten_kernel,
        in_specs=[VMEM_SPEC] * 7 + [HBM_SPEC],
        out_specs=[VMEM_SPEC] * 4,
        out_shape=(
            pltpu.VMEM((BLOCKS, rows, 2 * LANES), F32),
            pltpu.VMEM((BLOCKS + 1, HELD, 2 * LANES), BF16),
            pltpu.VMEM((WINS * OWN, LANES), F32),
            pltpu.VMEM((BLOCKS, 2 * LANES, LAGS), BF16),
        ),
        scratch_shapes=[
            pltpu.VMEM((4, rows, LENGTH // 4), BF16),
            pltpu.VMEM((rows, BINS), BF16),
            pltpu.SemaphoreType.DMA(()),
        ],
        compiler_params=limit,
    )(
        *(in_vmem(value) for value in (own, pair, *nexts, table, bands)),
        in_hbm(inverse_table()),
    )
    received = lax.ppermute(send, "core", [(0, 1), (1, 0)])
    scratch = [
        pltpu.VMEM((BLOCKS, HELD, 2 * LANES), F32),
        pltpu.VMEM((BLOCKS, HELD, LANES), F32),
        pltpu.VMEM((BLOCKS, 8 * OWN, 2 * LANES), BF16),
    ]
    own_lags = pl.pallas_call(
        own_kernel,
        in_specs=[VMEM_SPEC] * 4,
        out_specs=VMEM_SPEC,
        out_shape=pltpu.VMEM((8, OWN, LAGS), BF16),
        scratch_shapes=scratch,
        compiler_params=limit,
    )(*(in_vmem(value) for value in (send, ready, flags, inverse)))
    return pl.pallas_call(
        other_kernel,
        out_shape=jax.ShapeDtypeStruct((OWN, OWN, LAGS), BF16),
        in_specs=[VMEM_SPEC] * 5,
        scratch_shapes=scratch,
        compiler_params=limit,
    )(*(in_vmem(value) for value in (received, ready, flags, inverse, own_lags)))


def solution(mesh):
    split = Mesh(mesh.devices.reshape(4, 4, 2, 4, 2), ("x", "z", "core", "y", "zh"))
    recv, win = ("x", "z", "core"), ("y", "zh")
    in_specs = (P(recv, win, None), P(recv, win), P())
    out_specs = P(win, recv, None)
    return jax.shard_map(local, mesh=split, in_specs=in_specs, out_specs=out_specs, check_vma=False)
```

```python
import functools
import math

import jax
import jax.numpy as jnp
import numpy as np
from jax import lax
from jax.experimental import pallas as pl
from jax.experimental.pallas import tpu as pltpu
from jax.sharding import Mesh
from jax.sharding import PartitionSpec as P

LENGTH = 2048
BINS = LENGTH // 2
HALF = 256
LAGS = 2 * HALF
SMOOTH = 32
LANES = 128
SLICES = LENGTH // LANES
BLOCKS = BINS // LANES
WINS = 8
OWN = 16
SOURCES = 128
CHANNELS = 512
HELD = WINS * 8
EIGHTH = 0.70703125
MARK = 1e30
MARK_LIMIT = 1e29
BF16 = jnp.bfloat16
VMEM_SPEC = pl.BlockSpec(memory_space=pltpu.VMEM)
HBM_SPEC = pl.BlockSpec(memory_space=pltpu.HBM)
F32 = jnp.float32


def bin_order():
    low = np.arange(BINS // 4)
    order = np.stack([low, BINS // 2 - low, BINS // 2 + low, BINS - low])
    order[1, 0], order[3, 0] = BINS // 4, 3 * BINS // 4
    return order.reshape(-1)


def forward_table():
    samples = np.arange(LENGTH).reshape(LENGTH // 4, 4).T[:, :, None]
    bins = np.arange(BINS // 4)[None, None, :]
    phases = (samples * bins % LENGTH).astype(np.float32) * np.float32(2.0 * math.pi / LENGTH)
    real, imag = np.cos(phases), -np.sin(phases)
    imag[:, :, 0] = 1 - 2 * (np.arange(LENGTH // 4) % 2)
    table = np.stack([real, imag], axis=2).reshape(4, LENGTH // 4, 2, 2, LANES)
    return table.transpose(3, 0, 1, 2, 4).reshape(8, LENGTH // 4, 2 * LANES).astype(jnp.bfloat16)


def inverse_table():
    bins = bin_order()[:, None]
    lags = np.arange(LAGS)[None, :] - HALF
    phases = (bins * lags % LENGTH).astype(np.float32) * np.float32(2.0 * math.pi / LENGTH)
    factor = np.where(bins == 0, 1.0, 2.0).astype(np.float32) / np.float32(math.sqrt(LENGTH))
    table = np.stack([factor * np.cos(phases), -factor * np.sin(phases)], axis=0)
    table = table.reshape(2, BLOCKS, LANES, LAGS).transpose(1, 0, 2, 3)
    return table.reshape(BLOCKS, 2 * LANES, LAGS).astype(jnp.bfloat16)


def centre_kernel(records_ref, usable_ref, slices_ref, rows_ref):
    widened = records_ref[...].astype(F32)
    mean = jnp.sum(widened, axis=1, keepdims=True) * (1.0 / LENGTH)
    centred = widened - mean
    row_ids = lax.broadcasted_iota(jnp.int32, (OWN, OWN), 0)
    col_ids = lax.broadcasted_iota(jnp.int32, (OWN, OWN), 1)
    flags = jnp.broadcast_to(usable_ref[...].astype(F32), (OWN, OWN))
    flag = jnp.sum(jnp.where(row_ids == col_ids, flags, 0.0), axis=1, keepdims=True)
    marked = jnp.where(flag > 0.5, centred, MARK).astype(BF16)
    wide = 4 * LANES
    from_ids = lax.broadcasted_iota(jnp.int32, (wide, wide), 0)
    to_ids = lax.broadcasted_iota(jnp.int32, (wide, wide), 1)
    taken = 4 * lax.rem(to_ids, LANES) + lax.div(to_ids, LANES)
    move = (from_ids == taken).astype(F32).astype(BF16)
    marked = jnp.concatenate(
        [
            jnp.dot(marked[:, p : p + wide], move, preferred_element_type=F32).astype(BF16)
            for p in range(0, LENGTH, wide)
        ],
        axis=1,
    )
    rows_ref[...] = marked
    for part in range(SLICES):
        piece = marked[:, part * LANES : (part + 1) * LANES]
        slices_ref[2 * part] = piece
        slices_ref[2 * part + 1] = piece


def pick_kernel(sources_ref, all_ref, rows_ref, opposite_ref, picked_ref, pair_ref, token_ref):
    pair_ref[:OWN] = rows_ref[...]
    pair_ref[OWN:] = opposite_ref[...]
    core = lax.axis_index("core")
    rows = all_ref[...].reshape(CHANNELS, LANES)
    row_ids = lax.broadcasted_iota(jnp.int32, (HELD, SOURCES), 0)
    source_ids = lax.broadcasted_iota(jnp.int32, (HELD, SOURCES), 1)
    here = source_ids == lax.div(row_ids, 8) * 16 + core * 8 + lax.rem(row_ids, 8)
    wanted = jnp.sum(jnp.where(here, sources_ref[...].astype(F32), 0.0), axis=1, keepdims=True)
    channel_ids = lax.broadcasted_iota(jnp.int32, (HELD, CHANNELS), 1)
    onehot = (channel_ids == wanted.astype(jnp.int32)).astype(F32).astype(BF16)
    half = jnp.dot(onehot, rows, preferred_element_type=F32).astype(BF16).reshape(WINS, 8, LANES)
    for place in range(SLICES):
        picked_ref[pl.ds(place * WINS, WINS)] = half
    token_ref[...] = jnp.zeros((8, LANES), F32)


def bins_of(group, slot):
    if group % 2 == 0:
        return slot + group * (BINS // 4)
    return jnp.where(slot == 0, group * (BINS // 4), (group + 1) * (BINS // 4) - slot)


BANDS = ((0, 0), (1, 1), (0, 1), (1, 0), (1, 2))
REPEATS = ((2, 2), (3, 3), (2, 3), (3, 2))


def band_tile(pair):
    rows = lax.broadcasted_iota(jnp.int32, (2 * LANES, 2 * LANES), 0)
    cols = lax.broadcasted_iota(jnp.int32, (2 * LANES, 2 * LANES), 1)
    apart = jnp.abs(bins_of(pair[0], rows) - bins_of(pair[1], cols))
    return (apart <= SMOOTH).astype(F32).astype(BF16)


def load_kernel(token_ref, table_hbm, table_ref, bands_ref, sem):
    del token_ref
    copy = pltpu.make_async_copy(table_hbm, table_ref, sem)
    copy.start()
    for place, pair in enumerate(BANDS):
        bands_ref[place] = band_tile(pair)
    copy.wait()


def unmark(values):
    widened = values.astype(F32)
    return jnp.where(widened > MARK_LIMIT, 0.0, widened).astype(BF16)


def usable_lanes(values):
    return (values.astype(F32) < MARK_LIMIT).astype(F32)


def whiten(classes, table, bands, spec, amp):
    first = lax.broadcasted_iota(jnp.int32, (1, LANES), 1) == 0
    for block in range(2):
        parts = [jnp.dot(classes[r], table[4 * block + r], preferred_element_type=F32) for r in range(4)]
        real = [part[:, :LANES] for part in parts]
        imag = [part[:, LANES:] for part in parts]
        sum02_re, sum02_im, gap02_re, gap02_im = real[0] + real[2], imag[0] + imag[2], real[0] - real[2], imag[0] - imag[2]
        sum13_re, sum13_im, gap13_re, gap13_im = real[1] + real[3], imag[1] + imag[3], real[1] - real[3], imag[1] - imag[3]
        bins = [
            (sum02_re + sum13_re, sum02_im + sum13_im),
            (gap02_re - gap13_im, -gap02_im - gap13_re),
            (gap02_re + gap13_im, gap02_im - gap13_re),
            (sum02_re - sum13_re, sum13_im - sum02_im),
        ]
        if block == 0:
            gap, both = EIGHTH * gap13_im, EIGHTH * sum13_im
            special = [
                (bins[0][0], jnp.zeros_like(gap)),
                (imag[0] + gap, -imag[2] - both),
                (gap02_re, -gap13_re),
                (imag[0] - gap, imag[2] - both),
            ]
            bins = [
                tuple(jnp.where(first, new, old) for new, old in zip(at_first, at_rest))
                for at_first, at_rest in zip(special, bins)
            ]
        for group, (re, im) in enumerate(bins):
            place = 2 * group + block
            spec[place, :, :LANES] = re
            spec[place, :, LANES:] = im
            amp[:, pl.ds(place * LANES, LANES)] = jnp.sqrt(re * re + im * im).astype(BF16)

    tiles = {pair: bands[place] for place, pair in enumerate(BANDS)}
    tiles.update({pair: bands[place] for place, pair in enumerate(REPEATS)})
    tiles[2, 1] = band_tile((2, 1))
    wide_ids = lax.broadcasted_iota(jnp.int32, (1, 2 * LANES), 1)
    for group in range(4):
        total = None
        for other in range(4):
            if (other, group) in tiles:
                near = jnp.dot(
                    amp[:, pl.ds(other * 2 * LANES, 2 * LANES)],
                    tiles[other, group],
                    preferred_element_type=F32,
                )
                total = near if total is None else total + near
        bin_ids = bins_of(group, wide_ids)
        count = jnp.minimum(bin_ids, SMOOTH) + jnp.minimum(BINS - 1 - bin_ids, SMOOTH) + 1
        scale = 1.0 / (total * (1.0 / count.astype(F32)) + 1e-6)
        for half in range(2):
            block = 2 * group + half
            piece = scale[:, half * LANES : (half + 1) * LANES]
            spec[block, :, :LANES] = spec[block, :, :LANES] * piece
            spec[block, :, LANES:] = spec[block, :, LANES:] * piece


def whiten_kernel(
    own_ref, pair_ref, next1_ref, next2_ref, next3_ref, table, bands, inverse_hbm,
    spec, send, flags, inverse, classes, amp, sem,
):
    inverse_copy = pltpu.make_async_copy(inverse_hbm, inverse, sem)
    inverse_copy.start()
    line = lax.axis_index("y")
    side = lax.axis_index("zh")
    for part in range(SLICES):
        lanes = pl.ds(part // 4 * LANES, LANES)
        classes[part % 4, pl.ds(0, HELD), lanes] = unmark(own_ref[part].reshape(HELD, LANES))
    for step, ref in enumerate((pair_ref, next1_ref, next2_ref, next3_ref)):
        for swap in range(2):
            win = lax.rem(line + step, 4) * 2 + lax.rem(side + swap, 2)
            first = pl.multiple_of(win * OWN, OWN)
            where = pl.ds(HELD + first, OWN)
            received = ref[swap * OWN : swap * OWN + OWN, :]
            for part in range(SLICES):
                lanes = pl.ds(part // 4 * LANES, LANES)
                classes[part % 4, where, lanes] = unmark(received[:, part * LANES : (part + 1) * LANES])
            flags[pl.ds(first, OWN), :] = usable_lanes(received[:, :LANES])
    whiten(classes, table, bands, spec, amp)
    send[:BLOCKS] = spec[:, :HELD, :].astype(BF16)
    usable = usable_lanes(own_ref[0].reshape(HELD, LANES)).astype(BF16)
    send[BLOCKS, :, :LANES] = usable
    send[BLOCKS, :, LANES:] = usable
    inverse_copy.wait()


def correlate(sources, flags, ready, rec_flags, inverse, store, held, added, cross):
    held[...] = sources[:BLOCKS].astype(F32)
    added[...] = held[:, :, :LANES] + held[:, :, LANES:]

    def one_block(block, carry):
        for part in range(0, OWN, 8):
            rows = [pl.ds(HELD + w * OWN + part, 8) for w in range(WINS)]
            rec_re = [ready[block, where, :LANES] for where in rows]
            rec_im = [ready[block, where, LANES:] for where in rows]
            rec_sum = [re + im for re, im in zip(rec_re, rec_im)]
            rec_gap = [re - im for re, im in zip(rec_re, rec_im)]
            for index in range(8):
                sums = [None, None, None]
                for w in range(WINS):
                    row = w * 8 + index
                    src_re = jnp.broadcast_to(held[block, row : row + 1, :LANES], (8, LANES))
                    src_im = jnp.broadcast_to(held[block, row : row + 1, LANES:], (8, LANES))
                    src_sum = jnp.broadcast_to(added[block, row : row + 1, :], (8, LANES))
                    terms = (src_sum * rec_re[w], src_im * rec_gap[w], src_re * rec_sum[w])
                    sums = [term if acc is None else acc + term for acc, term in zip(sums, terms)]
                where = pl.ds(index * OWN + part, 8)
                cross[block, where, :LANES] = (sums[0] - sums[1]).astype(BF16)
                cross[block, where, LANES:] = (sums[0] - sums[2]).astype(BF16)
        return carry

    lax.fori_loop(0, BLOCKS, one_block, 0, unroll=True)
    lagged = jnp.dot(cross[0], inverse[0], preferred_element_type=F32)
    for block in range(1, BLOCKS):
        lagged += jnp.dot(cross[block], inverse[block], preferred_element_type=F32)
    for index in range(8):
        count = jnp.zeros((OWN, LANES), F32)
        for w in range(WINS):
            row = w * 8 + index
            source = jnp.broadcast_to(flags[row : row + 1, :], (OWN, LANES))
            count += source * rec_flags[w * OWN : w * OWN + OWN, :]
        scale = lax.rsqrt(jnp.maximum(count, 1.0))
        for piece in range(LAGS // LANES):
            lanes = slice(piece * LANES, (piece + 1) * LANES)
            store(index, lanes, (lagged[index * OWN : index * OWN + OWN, lanes] * scale).astype(BF16))


def own_kernel(send, ready, rec_flags, inverse, own_lags, held, added, cross):
    def store(index, lanes, values):
        own_lags[index, :, lanes] = values

    usable = send[BLOCKS, :, :LANES].astype(F32)
    correlate(send, usable, ready, rec_flags, inverse, store, held, added, cross)


def other_kernel(received, ready, rec_flags, inverse, own_lags, out_ref, held, added, cross):
    core = lax.axis_index("core")
    out_ref[pl.ds(core * 8, 8)] = own_lags[...]

    def store(index, lanes, values):
        out_ref[(1 - core) * 8 + index, :, lanes] = values

    usable = received[BLOCKS, :, :LANES].astype(F32)
    correlate(received, usable, ready, rec_flags, inverse, store, held, added, cross)


def in_vmem(value):
    return pltpu.with_memory_space_constraint(value, pltpu.VMEM)


def in_hbm(value):
    return pltpu.with_memory_space_constraint(jnp.asarray(value), pltpu.HBM)


def local(records, usable, sources):
    rows_in = records.reshape(OWN, LENGTH)
    slices, rows = pl.pallas_call(
        centre_kernel,
        out_specs=[VMEM_SPEC] * 2,
        out_shape=(pltpu.VMEM((2 * SLICES, OWN, LANES), BF16), pltpu.VMEM((OWN, LENGTH), BF16)),
    )(rows_in, usable.reshape(1, OWN))
    all_channels = lax.cond(
        lax.axis_index("core") < 2, lambda v: lax.all_to_all(v, ("x", "z", "core"), 0, 0), lambda v: v, slices
    )
    opposite = lax.ppermute(rows, "zh", [(0, 1), (1, 0)])
    picked, pair, token = pl.pallas_call(
        pick_kernel,
        in_specs=[VMEM_SPEC] * 4,
        out_specs=[VMEM_SPEC] * 3,
        out_shape=(
            pltpu.VMEM((SLICES * WINS, 8, LANES), BF16),
            pltpu.VMEM((2 * OWN, LENGTH), BF16),
            pltpu.VMEM((8, LANES), F32),
        ),
    )(sources.reshape(1, SOURCES), in_vmem(all_channels), in_vmem(rows), in_vmem(opposite))
    table, bands = pl.pallas_call(
        load_kernel,
        in_specs=[VMEM_SPEC, HBM_SPEC],
        out_specs=[VMEM_SPEC] * 2,
        out_shape=(
            pltpu.VMEM((8, LENGTH // 4, 2 * LANES), BF16),
            pltpu.VMEM((5, 2 * LANES, 2 * LANES), BF16),
        ),
        scratch_shapes=[pltpu.SemaphoreType.DMA(())],
        compiler_params=pltpu.CompilerParams(vmem_limit_bytes=2**20),
    )(token, in_hbm(forward_table()))
    nexts = [lax.ppermute(pair, "y", [(i, (i - k) % 4) for i in range(4)]) for k in (1, 2, 3)]
    own = lax.all_to_all(picked, ("x", "z", "y", "zh"), 0, 0)
    own, nexts, table, bands = lax.optimization_barrier((own, nexts, table, bands))
    own = own.reshape(SLICES, WINS, 8, LANES)
    rows = HELD + WINS * OWN
    limit = pltpu.CompilerParams(vmem_limit_bytes=16 * 2**20)
    ready, send, flags, inverse = pl.pallas_call(
        whiten_kernel,
        in_specs=[VMEM_SPEC] * 7 + [HBM_SPEC],
        out_specs=[VMEM_SPEC] * 4,
        out_shape=(
            pltpu.VMEM((BLOCKS, rows, 2 * LANES), F32),
            pltpu.VMEM((BLOCKS + 1, HELD, 2 * LANES), BF16),
            pltpu.VMEM((WINS * OWN, LANES), F32),
            pltpu.VMEM((BLOCKS, 2 * LANES, LAGS), BF16),
        ),
        scratch_shapes=[
            pltpu.VMEM((4, rows, LENGTH // 4), BF16),
            pltpu.VMEM((rows, BINS), BF16),
            pltpu.SemaphoreType.DMA(()),
        ],
        compiler_params=limit,
    )(
        *(in_vmem(value) for value in (own, pair, *nexts, table, bands)),
        in_hbm(inverse_table()),
    )
    received = lax.ppermute(send, "core", [(0, 1), (1, 0)])
    scratch = [
        pltpu.VMEM((BLOCKS, HELD, 2 * LANES), F32),
        pltpu.VMEM((BLOCKS, HELD, LANES), F32),
        pltpu.VMEM((BLOCKS, 8 * OWN, 2 * LANES), BF16),
    ]
    own_lags = pl.pallas_call(
        own_kernel,
        in_specs=[VMEM_SPEC] * 4,
        out_specs=VMEM_SPEC,
        out_shape=pltpu.VMEM((8, OWN, LAGS), BF16),
        scratch_shapes=scratch,
        compiler_params=limit,
    )(*(in_vmem(value) for value in (send, ready, flags, inverse)))
    return pl.pallas_call(
        other_kernel,
        out_shape=jax.ShapeDtypeStruct((OWN, OWN, LAGS), BF16),
        in_specs=[VMEM_SPEC] * 5,
        scratch_shapes=scratch,
        compiler_params=limit,
    )(*(in_vmem(value) for value in (received, ready, flags, inverse, own_lags)))


def solution(mesh):
    split = Mesh(mesh.devices.reshape(4, 4, 2, 4, 2), ("x", "z", "core", "y", "zh"))
    recv, win = ("x", "z", "core"), ("y", "zh")
    in_specs = (P(recv, win, None), P(recv, win), P())
    out_specs = P(win, recv, None)
    return jax.shard_map(local, mesh=split, in_specs=in_specs, out_specs=out_specs, check_vma=False)
```
